512 devices in a mesh: row: 64 (over z, x, core), col: 8 (over y).
Axes of the slice: x: 4, y: 8, z: 8, core: 2. Of those that a mesh axis runs over, the one named last changes fastest.
Arguments:
- noise: bfloat16 [32768, 512], P('row', 'col'), may hold values from -7 to 7
- data: bfloat16 [16384, 512], P(('col', 'row')), may hold values from -7 to 7
Outputs:
- targets: bfloat16 [32768, 512], P('row', 'col')
The draws below stay inside these ranges and needn't reach their ends.
All inputs are finite; a program needn't handle non-finite values.
Results may differ from the reference program's by a relative error of at most 0.015.
Values may be sent and summed in bfloat16 or wider, within the bound.
No kernel may reach another device: no remote copies, remote signals or barrier semaphores. Data moves between devices by JAX's collectives and lax.ppermute only.
A program may use at most 64 MiB of HBM per device.

```python
import math
import jax
import jax.numpy as jnp
from jax import lax

D = 512
ITERS = 4
NOISE = 32768
DATA = 16384


def latent_rows(key, rows, width):
    first, second = jax.random.split(key)
    base = jnp.clip(jax.random.normal(first, (rows, width), jnp.float32), -4.0, 4.0)
    scale = jnp.exp(jax.random.uniform(second, (rows, 1), jnp.float32, math.log(0.7), math.log(1.4)))
    return base * scale


def draw_noise(key, part):
    key = jax.random.fold_in(key, 11)
    return latent_rows(key, NOISE, D).astype(jnp.bfloat16)


def draw_data(key, part):
    key = jax.random.fold_in(key, 23)
    return latent_rows(key, DATA, D).astype(jnp.bfloat16)


def setup_inputs(seed: int = 0) -> dict:
    key_list = jax.random.split(jax.random.key(seed), 3)
    noise = draw_noise(jax.random.fold_in(key_list[2], 71), 0)
    data = draw_data(jax.random.fold_in(key_list[2], 71), 0)
    return {"noise": noise, "data": data}


eps_reg = 0.01


def cost_tile(rows, data, data_sq):
    cross = jnp.dot(rows, data.T, preferred_element_type=jnp.float32)
    rows_f = rows.astype(jnp.float32)
    rows_sq = jnp.sum(rows_f * rows_f, axis=1)
    return (rows_sq[:, None] + data_sq[None, :] - 2.0 * cross) / D


def reference(noise, data):
    block = math.gcd(NOISE, 1024)
    count = NOISE // block
    noise_blocks = noise.reshape(count, block, D)
    data_f = data.astype(jnp.float32)
    data_sq = jnp.sum(data_f * data_f, axis=1)
    f_pot = jnp.zeros((NOISE,), jnp.float32)
    g_pot = jnp.zeros((DATA,), jnp.float32)
    row_lse = jnp.zeros((NOISE,), jnp.float32)
    for sweep in range(ITERS):
        f_blocks = f_pot.reshape(count, block)

        def col_step(carry, item):
            top, total = carry
            rows, f_part = item
            scores = (f_part[:, None] - cost_tile(rows, data, data_sq)) / eps_reg
            newtop = jnp.maximum(top, jnp.max(scores, axis=0))
            total = total * jnp.exp(top - newtop) + jnp.sum(jnp.exp(scores - newtop[None, :]), axis=0)
            return (newtop, total), None

        init = (jnp.full((DATA,), -jnp.inf, jnp.float32), jnp.zeros((DATA,), jnp.float32))
        (top, total), unused = lax.scan(col_step, init, (noise_blocks, f_blocks))
        g_pot = -eps_reg * math.log(DATA) - eps_reg * (top + jnp.log(total))

        def row_step(rows):
            scores = (g_pot[None, :] - cost_tile(rows, data, data_sq)) / eps_reg
            peak = jnp.max(scores, axis=1)
            return peak + jnp.log(jnp.sum(jnp.exp(scores - peak[:, None]), axis=1))

        row_lse = lax.map(row_step, noise_blocks).reshape(NOISE)
        f_pot = -eps_reg * math.log(NOISE) - eps_reg * row_lse

    def target_step(item):
        rows, lse_part = item
        scores = (g_pot[None, :] - cost_tile(rows, data, data_sq)) / eps_reg
        weights = jnp.exp(scores - lse_part[:, None]).astype(jnp.bfloat16)
        return jnp.dot(weights, data, preferred_element_type=jnp.float32).astype(jnp.bfloat16)

    result = lax.map(target_step, (noise_blocks, row_lse.reshape(count, block)))
    return result.reshape(NOISE, D)
```

```python
import functools
import math

import jax
import jax.numpy as jnp
from jax import lax
from jax.experimental import pallas as pl
from jax.experimental.pallas import tpu as pltpu
from jax.sharding import PartitionSpec as P

ITERS = 4
EPS = 0.01
CORES, XS = 2, 4
SHIFT = 24.0 * math.log(2.0)
SCALE = 2.0**48
F32, BF16 = jnp.float32, jnp.bfloat16
VM = pl.BlockSpec(memory_space=pltpu.VMEM)


def params(mib):
    return pltpu.CompilerParams(vmem_limit_bytes=mib * 2**20)


def in_vmem(shape, dtype):
    return pltpu.VMEM(shape, dtype)


def call(body, outs, count, scratch=(), mib=32, name=None):
    return pl.pallas_call(
        body,
        out_shape=outs,
        in_specs=[VM] * count,
        out_specs=jax.tree.map(lambda _: VM, outs, is_leaf=lambda o: hasattr(o, "dtype")),
        scratch_shapes=list(scratch),
        compiler_params=params(mib),
        name=name,
    )


def lanes_to_rows(vec, out_ref):
    for r in range(vec.shape[0]):
        block = jnp.broadcast_to(vec[r : r + 1, :], (128, 128))
        out_ref[r * 128 : (r + 1) * 128, :] = block.T


def rows_to_lanes(ref):
    parts = []
    for r in range(ref.shape[0] // 128):
        parts.append(jnp.sum(ref[r * 128 : (r + 1) * 128, :].T, axis=0, keepdims=True))
    return jnp.concatenate(parts, axis=0)


def flat(vec):
    return jnp.concatenate([vec[t : t + 1, :] for t in range(vec.shape[0])], axis=1)


def lane_sum(val):
    total = val[:, 0:128]
    for t in range(1, val.shape[1] // 128):
        total = total + val[:, t * 128 : (t + 1) * 128]
    return total


def parts_of(refs):
    parts = []
    for ref in refs:
        if len(ref.shape) == 3:
            parts += [ref[k] for k in range(ref.shape[0])]
        else:
            parts.append(ref[...])
    return parts


def merged(refs):
    parts = parts_of(refs)
    top = functools.reduce(jnp.maximum, parts)
    return top + jnp.log(sum(jnp.exp(part - top) for part in parts))


def added(refs):
    return functools.reduce(jnp.add, parts_of(refs))


def noise_body(parts, out):
    for r in range(out.shape[0] // 128):
        at = slice(r * 128, (r + 1) * 128)
        block = jnp.concatenate(
            [parts[k, :, at].astype(F32).T for k in range(parts.shape[0])], axis=1
        )
        out[at, :] = block.astype(BF16)


def half_at(flip, rows):
    return pl.multiple_of(lax.rem(lax.axis_index("c") + flip, 2) * rows, rows)


def cost_body(own, far, data, score, lse, sq):
    rows, depth = own.shape
    width = 256
    ones = jnp.ones((8, depth), BF16)
    contract = (((1,), (1,)), ((), ()))
    for flip, noise in enumerate((own, far)):
        for r in range(rows // 128):
            block = noise[r * 128 : (r + 1) * 128, :].astype(F32)
            total = jnp.sum(lane_sum(block * block), axis=1, keepdims=True)
            sq[flip, r * 128 : (r + 1) * 128, :] = jnp.broadcast_to(total, (128, 128))
    for b in range(data.shape[0] // width):
        at = slice(b * width, (b + 1) * width)
        piece = data[at, :]
        wide = piece.astype(F32)
        square = wide * wide
        high = square.astype(BF16)
        low = (square - high.astype(F32)).astype(BF16)
        piece_sq = lax.dot_general(ones, high, contract, preferred_element_type=F32)
        piece_sq += lax.dot_general(ones, low, contract, preferred_element_type=F32)
        vals, tops = [], []
        for flip, noise in enumerate((own, far)):
            cross = lax.dot_general(noise[...], piece, contract, preferred_element_type=F32)
            rows_sq = jnp.concatenate([sq[flip]] * (width // 128), axis=1)
            val = (2.0 * cross - rows_sq - piece_sq[0:1, :]) * (1.0 / (depth * EPS))
            score[pl.ds(half_at(flip, rows), rows), at] = val
            vals.append(val)
            tops.append(jnp.max(val, axis=0, keepdims=True))
        top = jnp.maximum(tops[0], tops[1])
        total = sum(jnp.sum(jnp.exp(val - top), axis=0, keepdims=True) for val in vals)
        part = top + jnp.log(total)
        for t in range(width // 128):
            row = b * (width // 128) + t
            lse[row : row + 1, :] = part[:, t * 128 : (t + 1) * 128]


def first_row_body(log_data, n, *refs):
    parts, (score, expd, peak, lse, part, tops) = refs[:n], refs[n:]
    pot = flat(-log_data - merged(parts))
    rows = expd.shape[0]
    step = 32

    def body(r, carry):
        at = pl.ds(pl.multiple_of(r * step, step), step)
        val = score[at, :] + pot
        top = jnp.max(val, axis=1, keepdims=True)
        e = jnp.exp(val - (top - SHIFT))
        expd[at, :] = e
        part[at, :] = lane_sum(e)
        tops[at, :] = jnp.broadcast_to(top, (step, 128))
        return carry

    lax.fori_loop(0, rows // step, body, 0)
    sums = rows_to_lanes(part)
    high = jnp.concatenate(
        [tops[r * 128 : (r + 1) * 128, :].T[0:1, :] for r in range(rows // 128)], axis=0
    )
    peak[...] = high
    lse[...] = high + (jnp.log(sums) - SHIFT)


def column_sums(expd, factor, factors, out):
    lanes_to_rows(factor, factors)
    rows, cols = expd.shape
    copies = cols // 128

    def body(r, acc):
        at = pl.ds(pl.multiple_of(r * 8, 8), 8)
        f = factors[at, :]
        return acc + expd[at, :] * jnp.concatenate([f] * copies, axis=1)

    acc = lax.fori_loop(0, rows // 8, body, jnp.zeros((8, cols), F32), unroll=4)
    sums = jnp.sum(acc, axis=0, keepdims=True)
    count, width = out.shape
    for t in range(count):
        out[t : t + 1, :] = sums[:, t * width : (t + 1) * width]


def first_col_body(count, n, *refs):
    parts, (peak, expd, out, scale, factor, factors) = refs[:n], refs[n:]
    lse = merged(parts)
    s = jnp.exp(peak[...] - lse + SHIFT)
    scale[...] = s
    f = s * (1.0 / count)
    factor[...] = f
    column_sums(expd, f, factors, out)


def col_body(count, n, *refs):
    parts, (scale, expd, out, factor, factors) = refs[:n], refs[n:]
    f = scale[...] * ((SCALE / count) / added(parts))
    factor[...] = f
    column_sums(expd, f, factors, out)


def row_body(count, n, *refs):
    parts, (scale, expd, out, part) = refs[:n], refs[n:]
    v = jnp.broadcast_to(flat((SCALE / count) / added(parts)), (8, expd.shape[1]))
    rows = expd.shape[0]

    def body(r, carry):
        at = pl.ds(pl.multiple_of(r * 8, 8), 8)
        part[at, :] = lane_sum(expd[at, :] * v)
        return carry

    lax.fori_loop(0, rows // 8, body, 0, unroll=4)
    out[...] = rows_to_lanes(part) * scale[...]


def split_three(mass, deep):
    high = mass.astype(BF16)
    rest = mass - high.astype(F32)
    mid = rest.astype(BF16)
    low = (rest - mid.astype(F32)).astype(BF16)
    zero = jnp.zeros((deep - 3, mass.shape[1]), BF16)
    return jnp.concatenate([high, mid, low, zero], axis=0)


def add_three(tail):
    return tail[0:1, :] + tail[1:2, :] + tail[2:3, :]


def target_body(count, flip, n, *refs):
    parts, (factor, expd, data, out) = refs[:n], refs[n : n + 4]
    *mass, part, factors, weights = refs[n + 4 :]
    v = jnp.broadcast_to(flat((SCALE / count) / added(parts)), (16, expd.shape[1]))
    rows, wide = weights.shape
    base = half_at(flip, rows)
    lanes_to_rows(factor[pl.ds(lax.rem(lax.axis_index("c") + flip, 2) * (rows // 128), rows // 128), :], factors)

    def body(r, carry):
        at = pl.ds(pl.multiple_of(r * 16, 16), 16)
        f = jnp.concatenate([factors[at, :]] * (wide // 128), axis=1)
        w = expd[pl.ds(pl.multiple_of(base + r * 16, 16), 16), :] * v * f
        part[at, :] = lane_sum(w)
        weights[at, :] = w.astype(BF16)
        return carry

    lax.fori_loop(0, rows // 16, body, 0, unroll=2)
    cols, deep, _ = out.shape
    depth = data.shape[1] // cols
    for r in range(rows // 128):
        at = slice(r * 128, (r + 1) * 128)
        block = jnp.dot(weights[at, :], data[...], preferred_element_type=F32)
        block = block.T.astype(out.dtype)
        for k in range(cols):
            out[k, 0:depth, at] = block[k * depth : (k + 1) * depth, :]
    sums = rows_to_lanes(part)
    if mass:
        mass[0][...] = sums
    else:
        tail = split_three(flat(sums), deep - depth)
        for k in range(cols):
            out[k, depth:deep, :] = tail


def pack_body(own, mass, far, out):
    depth, deep = own.shape[1], out.shape[1]
    total = flat(mass[...]) + add_three(far[0, depth:deep, :].astype(F32))
    tail = split_three(total, deep - depth)
    for k in range(out.shape[0]):
        out[k, 0:depth, :] = (own[k] + far[k, 0:depth, :].astype(F32)).astype(BF16)
        out[k, depth:deep, :] = tail


def finish_body(parts, out):
    depth, deep = out.shape[0], parts.shape[1]
    total = functools.reduce(jnp.add, [parts[k, 0:depth, :].astype(F32) for k in range(parts.shape[0])])
    tails = [parts[k, depth:deep, :].astype(F32) for k in range(parts.shape[0])]
    out[...] = (total / add_three(functools.reduce(jnp.add, tails))).astype(BF16)


def everyone(val, axes):
    count = lax.axis_size(axes)
    copies = jnp.broadcast_to(val[None], (count,) + val.shape)
    return lax.all_to_all(copies, axes, 0, 0, tiled=True)


def swapped(val):
    return lax.ppermute(val, "c", [(0, 1), (1, 0)])


def on_device(noise, data, *, vmem=in_vmem):
    zs, xs, cs, cols_all = (lax.axis_size(a) for a in ("z", "x", "c", "col"))
    half, slice_width = noise.shape
    rows = half * cs
    depth = slice_width * cols_all
    wide = data.shape[0] * zs * xs
    count_noise, count_data = float(rows * zs * xs), float(wide * cs * cols_all)
    log_data = math.log(count_data)
    row_axes, col_axes = ("z", "x"), ("col", "c")

    noise_parts = lax.all_gather(noise.T, "col", axis=0)
    stacked = everyone(data, "z").reshape(data.shape[0] * zs, depth)
    data_all = everyone(stacked, "x").reshape(wide, depth)
    own = call(noise_body, jax.ShapeDtypeStruct((half, depth), BF16), 1, name="noise")(noise_parts)
    far = swapped(own)

    vec_col = jax.ShapeDtypeStruct((wide // 128, 128), F32)
    vec_row = jax.ShapeDtypeStruct((rows // 128, 128), F32)
    tile = vmem((rows, wide), F32)
    strip = pltpu.VMEM((rows, 128), F32)

    score, lse = call(
        cost_body, (tile, vec_col), 3, [pltpu.VMEM((cs, half, 128), F32)], name="cost"
    )(own, far, data_all)
    parts = everyone(lse, row_axes)
    expd, peak, lse = call(
        functools.partial(first_row_body, log_data, 1),
        (tile, vec_row, vec_row), 2, [strip, strip], name="first_rows",
    )(parts, score)
    parts = everyone(lse, col_axes)
    sums, scale, factor = call(
        functools.partial(first_col_body, count_noise, 1),
        (vec_col, vec_row, vec_row), 3, [strip], name="first_cols",
    )(parts, peak, expd)
    for sweep in range(1, ITERS - 1):
        parts = everyone(sums, row_axes)
        mass = call(
            functools.partial(row_body, count_data, 1), vec_row, 3, [strip], name="rows"
        )(parts, scale, expd)
        parts = everyone(mass, col_axes)
        sums, factor = call(
            functools.partial(col_body, count_noise, 1), (vec_col, vec_row), 3, [strip], name="cols"
        )(parts, scale, expd)
    parts = everyone(sums, row_axes)

    strips = [pltpu.VMEM((half, 128), F32)] * 2 + [pltpu.VMEM((half, wide), BF16)]
    packed = jax.ShapeDtypeStruct((cols_all, slice_width + 16, half), BF16)
    far = call(
        functools.partial(target_body, count_data, 1, 1), packed, 4, strips, name="targets_far"
    )(parts, factor, expd, data_all)
    far = swapped(far)
    mine, mass = call(
        functools.partial(target_body, count_data, 0, 1),
        (vmem((cols_all, slice_width, half), F32), jax.ShapeDtypeStruct((half // 128, 128), F32)),
        4, strips, name="targets_own",
    )(parts, factor, expd, data_all)
    pieces = call(pack_body, packed, 3, name="pack")(mine, mass, far)
    got = lax.all_to_all(pieces, "col", 0, 0, tiled=True)
    out = call(finish_body, jax.ShapeDtypeStruct((slice_width, half), BF16), 1, name="finish")(got)
    return out.T


def solution(mesh):
    rows, cols = mesh.devices.shape
    parts = (rows // (XS * CORES), XS, CORES, cols)
    split = jax.sharding.Mesh(mesh.devices.reshape(parts), ("z", "x", "c", "col"))
    return jax.shard_map(
        on_device,
        mesh=split,
        in_specs=(P(("z", "x", "c"), "col"), P(("col", "z", "x", "c"), None)),
        out_specs=P(("z", "x", "c"), "col"),
        check_vma=False,
    )
```

```python
import functools
import math

import jax
import jax.numpy as jnp
from jax import lax
from jax.experimental import pallas as pl
from jax.experimental.pallas import tpu as pltpu
from jax.sharding import PartitionSpec as P

ITERS = 4
EPS = 0.01
CORES, XS = 2, 4
SHIFT = 24.0 * math.log(2.0)
SCALE = 2.0**48
F32, BF16 = jnp.float32, jnp.bfloat16
VM = pl.BlockSpec(memory_space=pltpu.VMEM)


def params(mib):
    return pltpu.CompilerParams(vmem_limit_bytes=mib * 2**20)


def in_vmem(shape, dtype):
    return pltpu.VMEM(shape, dtype)


def call(body, outs, count, scratch=(), mib=32, name=None):
    return pl.pallas_call(
        body,
        out_shape=outs,
        in_specs=[VM] * count,
        out_specs=jax.tree.map(lambda _: VM, outs, is_leaf=lambda o: hasattr(o, "dtype")),
        scratch_shapes=list(scratch),
        compiler_params=params(mib),
        name=name,
    )


def lanes_to_rows(vec, out_ref):
    for r in range(vec.shape[0]):
        block = jnp.broadcast_to(vec[r : r + 1, :], (128, 128))
        out_ref[r * 128 : (r + 1) * 128, :] = block.T


def rows_to_lanes(ref):
    parts = []
    for r in range(ref.shape[0] // 128):
        parts.append(jnp.sum(ref[r * 128 : (r + 1) * 128, :].T, axis=0, keepdims=True))
    return jnp.concatenate(parts, axis=0)


def flat(vec):
    return jnp.concatenate([vec[t : t + 1, :] for t in range(vec.shape[0])], axis=1)


def lane_sum(val):
    total = val[:, 0:128]
    for t in range(1, val.shape[1] // 128):
        total = total + val[:, t * 128 : (t + 1) * 128]
    return total


def parts_of(refs):
    parts = []
    for ref in refs:
        if len(ref.shape) == 3:
            parts += [ref[k] for k in range(ref.shape[0])]
        else:
            parts.append(ref[...])
    return parts


def merged(refs):
    parts = parts_of(refs)
    top = functools.reduce(jnp.maximum, parts)
    return top + jnp.log(sum(jnp.exp(part - top) for part in parts))


def added(refs):
    return functools.reduce(jnp.add, parts_of(refs))


def noise_body(parts, out):
    for r in range(out.shape[0] // 128):
        at = slice(r * 128, (r + 1) * 128)
        block = jnp.concatenate(
            [parts[k, :, at].astype(F32).T for k in range(parts.shape[0])], axis=1
        )
        out[at, :] = block.astype(BF16)


def half_at(flip, rows):
    return pl.multiple_of(lax.rem(lax.axis_index("c") + flip, 2) * rows, rows)


def cost_body(own, far, data, score, lse, sq):
    rows, depth = own.shape
    width = 256
    ones = jnp.ones((8, depth), BF16)
    contract = (((1,), (1,)), ((), ()))
    for flip, noise in enumerate((own, far)):
        for r in range(rows // 128):
            block = noise[r * 128 : (r + 1) * 128, :].astype(F32)
            total = jnp.sum(lane_sum(block * block), axis=1, keepdims=True)
            sq[flip, r * 128 : (r + 1) * 128, :] = jnp.broadcast_to(total, (128, 128))
    for b in range(data.shape[0] // width):
        at = slice(b * width, (b + 1) * width)
        piece = data[at, :]
        wide = piece.astype(F32)
        square = wide * wide
        high = square.astype(BF16)
        low = (square - high.astype(F32)).astype(BF16)
        piece_sq = lax.dot_general(ones, high, contract, preferred_element_type=F32)
        piece_sq += lax.dot_general(ones, low, contract, preferred_element_type=F32)
        vals, tops = [], []
        for flip, noise in enumerate((own, far)):
            cross = lax.dot_general(noise[...], piece, contract, preferred_element_type=F32)
            rows_sq = jnp.concatenate([sq[flip]] * (width // 128), axis=1)
            val = (2.0 * cross - rows_sq - piece_sq[0:1, :]) * (1.0 / (depth * EPS))
            score[pl.ds(half_at(flip, rows), rows), at] = val
            vals.append(val)
            tops.append(jnp.max(val, axis=0, keepdims=True))
        top = jnp.maximum(tops[0], tops[1])
        total = sum(jnp.sum(jnp.exp(val - top), axis=0, keepdims=True) for val in vals)
        part = top + jnp.log(total)
        for t in range(width // 128):
            row = b * (width // 128) + t
            lse[row : row + 1, :] = part[:, t * 128 : (t + 1) * 128]


def first_row_body(log_data, n, *refs):
    parts, (score, expd, peak, lse, part, tops) = refs[:n], refs[n:]
    pot = flat(-log_data - merged(parts))
    rows = expd.shape[0]
    step = 32

    def body(r, carry):
        at = pl.ds(pl.multiple_of(r * step, step), step)
        val = score[at, :] + pot
        top = jnp.max(val, axis=1, keepdims=True)
        e = jnp.exp(val - (top - SHIFT))
        expd[at, :] = e
        part[at, :] = lane_sum(e)
        tops[at, :] = jnp.broadcast_to(top, (step, 128))
        return carry

    lax.fori_loop(0, rows // step, body, 0)
    sums = rows_to_lanes(part)
    high = jnp.concatenate(
        [tops[r * 128 : (r + 1) * 128, :].T[0:1, :] for r in range(rows // 128)], axis=0
    )
    peak[...] = high
    lse[...] = high + (jnp.log(sums) - SHIFT)


def column_sums(expd, factor, factors, out):
    lanes_to_rows(factor, factors)
    rows, cols = expd.shape
    copies = cols // 128

    def body(r, acc):
        at = pl.ds(pl.multiple_of(r * 8, 8), 8)
        f = factors[at, :]
        return acc + expd[at, :] * jnp.concatenate([f] * copies, axis=1)

    acc = lax.fori_loop(0, rows // 8, body, jnp.zeros((8, cols), F32), unroll=4)
    sums = jnp.sum(acc, axis=0, keepdims=True)
    count, width = out.shape
    for t in range(count):
        out[t : t + 1, :] = sums[:, t * width : (t + 1) * width]


def first_col_body(count, n, *refs):
    parts, (peak, expd, out, scale, factor, factors) = refs[:n], refs[n:]
    lse = merged(parts)
    s = jnp.exp(peak[...] - lse + SHIFT)
    scale[...] = s
    f = s * (1.0 / count)
    factor[...] = f
    column_sums(expd, f, factors, out)


def col_body(count, n, *refs):
    parts, (scale, expd, out, factor, factors) = refs[:n], refs[n:]
    f = scale[...] * ((SCALE / count) / added(parts))
    factor[...] = f
    column_sums(expd, f, factors, out)


def row_body(count, n, *refs):
    parts, (scale, expd, out, part) = refs[:n], refs[n:]
    v = jnp.broadcast_to(flat((SCALE / count) / added(parts)), (8, expd.shape[1]))
    rows = expd.shape[0]

    def body(r, carry):
        at = pl.ds(pl.multiple_of(r * 8, 8), 8)
        part[at, :] = lane_sum(expd[at, :] * v)
        return carry

    lax.fori_loop(0, rows // 8, body, 0, unroll=4)
    out[...] = rows_to_lanes(part) * scale[...]


def split_three(mass, deep):
    high = mass.astype(BF16)
    rest = mass - high.astype(F32)
    mid = rest.astype(BF16)
    low = (rest - mid.astype(F32)).astype(BF16)
    zero = jnp.zeros((deep - 3, mass.shape[1]), BF16)
    return jnp.concatenate([high, mid, low, zero], axis=0)


def add_three(tail):
    return tail[0:1, :] + tail[1:2, :] + tail[2:3, :]


def target_body(count, flip, n, *refs):
    parts, (factor, expd, data, out) = refs[:n], refs[n : n + 4]
    *mass, part, factors, weights = refs[n + 4 :]
    v = jnp.broadcast_to(flat((SCALE / count) / added(parts)), (16, expd.shape[1]))
    rows, wide = weights.shape
    base = half_at(flip, rows)
    lanes_to_rows(factor[pl.ds(lax.rem(lax.axis_index("c") + flip, 2) * (rows // 128), rows // 128), :], factors)

    def body(r, carry):
        at = pl.ds(pl.multiple_of(r * 16, 16), 16)
        f = jnp.concatenate([factors[at, :]] * (wide // 128), axis=1)
        w = expd[pl.ds(pl.multiple_of(base + r * 16, 16), 16), :] * v * f
        part[at, :] = lane_sum(w)
        weights[at, :] = w.astype(BF16)
        return carry

    lax.fori_loop(0, rows // 16, body, 0, unroll=2)
    cols, deep, _ = out.shape
    depth = data.shape[1] // cols
    for r in range(rows // 128):
        at = slice(r * 128, (r + 1) * 128)
        block = jnp.dot(weights[at, :], data[...], preferred_element_type=F32)
        block = block.T.astype(out.dtype)
        for k in range(cols):
            out[k, 0:depth, at] = block[k * depth : (k + 1) * depth, :]
    sums = rows_to_lanes(part)
    if mass:
        mass[0][...] = sums
    else:
        tail = split_three(flat(sums), deep - depth)
        for k in range(cols):
            out[k, depth:deep, :] = tail


def pack_body(own, mass, far, out):
    depth, deep = own.shape[1], out.shape[1]
    total = flat(mass[...]) + add_three(far[0, depth:deep, :].astype(F32))
    tail = split_three(total, deep - depth)
    for k in range(out.shape[0]):
        out[k, 0:depth, :] = (own[k] + far[k, 0:depth, :].astype(F32)).astype(BF16)
        out[k, depth:deep, :] = tail


def finish_body(parts, out):
    depth, deep = out.shape[0], parts.shape[1]
    total = functools.reduce(jnp.add, [parts[k, 0:depth, :].astype(F32) for k in range(parts.shape[0])])
    tails = [parts[k, depth:deep, :].astype(F32) for k in range(parts.shape[0])]
    out[...] = (total / add_three(functools.reduce(jnp.add, tails))).astype(BF16)


def join_body(how, parts, out):
    out[...] = how([parts])


def everyone(val, axes):
    count = lax.axis_size(axes)
    copies = jnp.broadcast_to(val[None], (count,) + val.shape)
    return lax.all_to_all(copies, axes, 0, 0, tiled=True)


def joined(how, val):
    return call(functools.partial(join_body, how), jax.ShapeDtypeStruct(val.shape[1:], F32), 1, name="join")(val)


def by_axis(how, val, axes):
    for axis in axes[:-1]:
        val = joined(how, lax.all_gather(val, axis, axis=0))
    return lax.all_gather(val, axes[-1], axis=0)


def swapped(val):
    return lax.ppermute(val, "c", [(0, 1), (1, 0)])


def on_device(noise, data, *, vmem=in_vmem):
    zs, xs, cs, cols_all = (lax.axis_size(a) for a in ("z", "x", "c", "col"))
    half, slice_width = noise.shape
    rows = half * cs
    depth = slice_width * cols_all
    wide = data.shape[0] * zs * xs
    count_noise, count_data = float(rows * zs * xs), float(wide * cs * cols_all)
    log_data = math.log(count_data)
    row_axes, col_axes = ("z", "x"), ("col", "c")

    noise_parts = lax.all_gather(noise.T, "col", axis=0)
    data_all = everyone(data, ("z", "x")).reshape(wide, depth)
    own = call(noise_body, jax.ShapeDtypeStruct((half, depth), BF16), 1, name="noise")(noise_parts)
    far = swapped(own)

    vec_col = jax.ShapeDtypeStruct((wide // 128, 128), F32)
    vec_row = jax.ShapeDtypeStruct((rows // 128, 128), F32)
    tile = vmem((rows, wide), F32)
    strip = pltpu.VMEM((rows, 128), F32)

    score, lse = call(
        cost_body, (tile, vec_col), 3, [pltpu.VMEM((cs, half, 128), F32)], name="cost"
    )(own, far, data_all)
    parts = by_axis(merged, lse, ("z", "x"))
    expd, peak, lse = call(
        functools.partial(first_row_body, log_data, 1),
        (tile, vec_row, vec_row), 2, [strip, strip], name="first_rows",
    )(parts, score)
    parts = by_axis(merged, lse, ("c", "col"))
    sums, scale, factor = call(
        functools.partial(first_col_body, count_noise, 1),
        (vec_col, vec_row, vec_row), 3, [strip], name="first_cols",
    )(parts, peak, expd)
    for sweep in range(1, ITERS - 1):
        parts = by_axis(added, sums, ("x", "z")) if sweep == 2 else everyone(sums, row_axes)
        mass = call(
            functools.partial(row_body, count_data, 1), vec_row, 3, [strip], name="rows"
        )(parts, scale, expd)
        parts = by_axis(added, mass, ("col", "c")) if sweep == 2 else everyone(mass, col_axes)
        sums, factor = call(
            functools.partial(col_body, count_noise, 1), (vec_col, vec_row), 3, [strip], name="cols"
        )(parts, scale, expd)
    parts = everyone(sums, row_axes)

    strips = [pltpu.VMEM((half, 128), F32)] * 2 + [pltpu.VMEM((half, wide), BF16)]
    packed = jax.ShapeDtypeStruct((cols_all, slice_width + 16, half), BF16)
    far = call(
        functools.partial(target_body, count_data, 1, 1), packed, 4, strips, name="targets_far"
    )(parts, factor, expd, data_all)
    far = swapped(far)
    mine, mass = call(
        functools.partial(target_body, count_data, 0, 1),
        (vmem((cols_all, slice_width, half), F32), jax.ShapeDtypeStruct((half // 128, 128), F32)),
        4, strips, name="targets_own",
    )(parts, factor, expd, data_all)
    pieces = call(pack_body, packed, 3, name="pack")(mine, mass, far)
    got = lax.all_to_all(pieces, "col", 0, 0, tiled=True)
    out = call(finish_body, jax.ShapeDtypeStruct((slice_width, half), BF16), 1, name="finish")(got)
    return out.T


def solution(mesh):
    rows, cols = mesh.devices.shape
    parts = (rows // (XS * CORES), XS, CORES, cols)
    split = jax.sharding.Mesh(mesh.devices.reshape(parts), ("z", "x", "c", "col"))
    return jax.shard_map(
        on_device,
        mesh=split,
        in_specs=(P(("z", "x", "c"), "col"), P(("col", "z", "x", "c"), None)),
        out_specs=P(("z", "x", "c"), "col"),
        check_vma=False,
    )
```

```python
import functools
import math

import jax
import jax.numpy as jnp
from jax import lax
from jax.experimental import pallas as pl
from jax.experimental.pallas import tpu as pltpu
from jax.sharding import PartitionSpec as P

ITERS = 4
EPS = 0.01
CORES, XS = 2, 4
SHIFT = 24.0 * math.log(2.0)
SCALE = 2.0**48
F32, BF16 = jnp.float32, jnp.bfloat16
VM = pl.BlockSpec(memory_space=pltpu.VMEM)


def params(mib):
    return pltpu.CompilerParams(vmem_limit_bytes=mib * 2**20)


def in_vmem(shape, dtype):
    return pltpu.VMEM(shape, dtype)


def call(body, outs, count, scratch=(), mib=32, name=None):
    return pl.pallas_call(
        body,
        out_shape=outs,
        in_specs=[VM] * count,
        out_specs=jax.tree.map(lambda _: VM, outs, is_leaf=lambda o: hasattr(o, "dtype")),
        scratch_shapes=list(scratch),
        compiler_params=params(mib),
        name=name,
    )


def lanes_to_rows(vec, out_ref):
    for r in range(vec.shape[0]):
        block = jnp.broadcast_to(vec[r : r + 1, :], (128, 128))
        out_ref[r * 128 : (r + 1) * 128, :] = block.T


def rows_to_lanes(ref):
    parts = []
    for r in range(ref.shape[0] // 128):
        parts.append(jnp.sum(ref[r * 128 : (r + 1) * 128, :].T, axis=0, keepdims=True))
    return jnp.concatenate(parts, axis=0)


def flat(vec):
    return jnp.concatenate([vec[t : t + 1, :] for t in range(vec.shape[0])], axis=1)


def lane_sum(val):
    total = val[:, 0:128]
    for t in range(1, val.shape[1] // 128):
        total = total + val[:, t * 128 : (t + 1) * 128]
    return total


def parts_of(refs):
    parts = []
    for ref in refs:
        if len(ref.shape) == 3:
            parts += [ref[k] for k in range(ref.shape[0])]
        else:
            parts.append(ref[...])
    return parts


def merged(refs):
    parts = parts_of(refs)
    top = functools.reduce(jnp.maximum, parts)
    return top + jnp.log(sum(jnp.exp(part - top) for part in parts))


def added(refs):
    return functools.reduce(jnp.add, parts_of(refs))


def noise_body(parts, out, sq):
    cols, cores, depth, half = parts.shape
    for c in range(cores):
        for r in range(half // 128):
            at = slice(r * 128, (r + 1) * 128)
            total = jnp.zeros((1, 128), F32)
            blocks = []
            for k in range(cols):
                block = parts[k, c, :, at].astype(F32)
                total = total + jnp.sum(block * block, axis=0, keepdims=True)
                blocks.append(block.T)
            row = c * (half // 128) + r
            out[row * 128 : (row + 1) * 128, :] = jnp.concatenate(blocks, axis=1).astype(BF16)
            sq[row : row + 1, :] = total


def cost_body(noise, noise_sq, data, score, lse, rows_sq, part):
    rows, depth = noise.shape
    width, step = 256, min(rows, 512)
    contract = (((1,), (1,)), ((), ()))
    lanes_to_rows(noise_sq[...], rows_sq)
    for b in range(data.shape[0] // width):
        at = slice(b * width, (b + 1) * width)
        piece = data[at, :]
        wide = piece.astype(F32)
        part[at, :] = lane_sum(wide * wide)
        piece_sq = flat(rows_to_lanes(part.at[at, :]))
        tops = []
        for r in range(rows // step):
            here = slice(r * step, (r + 1) * step)
            cross = lax.dot_general(noise[here, :], piece, contract, preferred_element_type=F32)
            sq = jnp.concatenate([rows_sq[here, :]] * (width // 128), axis=1)
            val = (2.0 * cross - sq - piece_sq) * (1.0 / (depth * EPS))
            score[here, at] = val
            tops.append(jnp.max(val, axis=0, keepdims=True))
        top = functools.reduce(jnp.maximum, tops)
        total = jnp.sum(jnp.exp(score[:, at] - top), axis=0, keepdims=True)
        sums = top + jnp.log(total)
        for t in range(width // 128):
            row = b * (width // 128) + t
            lse[row : row + 1, :] = sums[:, t * 128 : (t + 1) * 128]


def first_row_body(log_data, n, *refs):
    parts, (score, expd, peak, lse, part, tops) = refs[:n], refs[n:]
    rows, cols = expd.shape
    pot = jnp.broadcast_to(flat(-log_data - merged(parts)), (8, cols))

    def find(r, carry):
        at = pl.ds(pl.multiple_of(r * 8, 8), 8)
        val = score[at, :] + pot
        part[at, :] = functools.reduce(
            jnp.maximum, [val[:, t * 128 : (t + 1) * 128] for t in range(cols // 128)]
        )
        return carry

    lax.fori_loop(0, rows // 8, find, 0, unroll=8)
    high = jnp.concatenate(
        [
            jnp.max(part[r * 128 : (r + 1) * 128, :].T, axis=0, keepdims=True)
            for r in range(rows // 128)
        ],
        axis=0,
    )
    lanes_to_rows(high - SHIFT, tops)

    def raise_up(r, carry):
        at = pl.ds(pl.multiple_of(r * 8, 8), 8)
        e = jnp.exp((score[at, :] + pot) - jnp.concatenate([tops[at, :]] * (cols // 128), axis=1))
        expd[at, :] = e
        part[at, :] = lane_sum(e)
        return carry

    lax.fori_loop(0, rows // 8, raise_up, 0, unroll=8)
    peak[...] = high
    lse[...] = high + (jnp.log(rows_to_lanes(part)) - SHIFT)


def column_sums(expd, factor, factors, out):
    lanes_to_rows(factor, factors)
    rows, cols = expd.shape
    copies = cols // 128

    def body(r, acc):
        at = pl.ds(pl.multiple_of(r * 8, 8), 8)
        f = factors[at, :]
        return acc + expd[at, :] * jnp.concatenate([f] * copies, axis=1)

    acc = lax.fori_loop(0, rows // 8, body, jnp.zeros((8, cols), F32), unroll=8)
    sums = jnp.sum(acc, axis=0, keepdims=True)
    count, width = out.shape
    for t in range(count):
        out[t : t + 1, :] = sums[:, t * width : (t + 1) * width]


def first_col_body(count, n, *refs):
    parts, (peak, expd, out, scale, factors) = refs[:n], refs[n:]
    s = jnp.exp(peak[...] - merged(parts) + SHIFT)
    scale[...] = s
    column_sums(expd, s * (1.0 / count), factors, out)


def col_body(count, n, *refs):
    parts, (scale, expd, out, *factor, factors) = refs[:n], refs[n:]
    f = scale[...] * ((SCALE / count) / added(parts))
    for ref in factor:
        ref[...] = f
    column_sums(expd, f, factors, out)


def row_body(count, n, *refs):
    parts, (scale, expd, out, part) = refs[:n], refs[n:]
    v = jnp.broadcast_to(flat((SCALE / count) / added(parts)), (8, expd.shape[1]))
    rows = expd.shape[0]

    def body(r, carry):
        at = pl.ds(pl.multiple_of(r * 8, 8), 8)
        part[at, :] = lane_sum(expd[at, :] * v)
        return carry

    lax.fori_loop(0, rows // 8, body, 0, unroll=8)
    out[...] = rows_to_lanes(part) * scale[...]


def half_at(flip, rows):
    return pl.multiple_of(lax.rem(lax.axis_index("c") + flip, 2) * rows, rows)


def split_three(mass, deep):
    high = mass.astype(BF16)
    rest = mass - high.astype(F32)
    mid = rest.astype(BF16)
    low = (rest - mid.astype(F32)).astype(BF16)
    zero = jnp.zeros((deep - 3, mass.shape[1]), BF16)
    return jnp.concatenate([high, mid, low, zero], axis=0)


def add_three(tail):
    return tail[0:1, :] + tail[1:2, :] + tail[2:3, :]


def target_body(count, flip, n, *refs):
    parts, (factor, expd, data, out) = refs[:n], refs[n : n + 4]
    *mass, part, factors, weights = refs[n + 4 :]
    v = jnp.broadcast_to(flat((SCALE / count) / added(parts)), (16, expd.shape[1]))
    rows, wide = weights.shape
    base = half_at(flip, rows)
    lanes_to_rows(factor[pl.ds(lax.rem(lax.axis_index("c") + flip, 2) * (rows // 128), rows // 128), :], factors)

    def body(r, carry):
        at = pl.ds(pl.multiple_of(r * 16, 16), 16)
        f = jnp.concatenate([factors[at, :]] * (wide // 128), axis=1)
        w = expd[pl.ds(pl.multiple_of(base + r * 16, 16), 16), :] * v * f
        part[at, :] = lane_sum(w)
        weights[at, :] = w.astype(BF16)
        return carry

    lax.fori_loop(0, rows // 16, body, 0, unroll=2)
    cols, deep, _ = out.shape
    depth = data.shape[1] // cols
    for r in range(rows // 128):
        at = slice(r * 128, (r + 1) * 128)
        block = jnp.dot(weights[at, :], data[...], preferred_element_type=F32)
        block = block.T.astype(out.dtype)
        for k in range(cols):
            out[k, 0:depth, at] = block[k * depth : (k + 1) * depth, :]
    sums = rows_to_lanes(part)
    if mass:
        mass[0][...] = sums
    else:
        tail = split_three(flat(sums), deep - depth)
        for k in range(cols):
            out[k, depth:deep, :] = tail


def pack_body(own, mass, far, out):
    depth, deep = own.shape[1], out.shape[1]
    total = flat(mass[...]) + add_three(far[0, depth:deep, :].astype(F32))
    tail = split_three(total, deep - depth)
    for k in range(out.shape[0]):
        out[k, 0:depth, :] = (own[k] + far[k, 0:depth, :].astype(F32)).astype(BF16)
        out[k, depth:deep, :] = tail


def finish_body(parts, out):
    depth, deep = out.shape[0], parts.shape[1]
    total = functools.reduce(jnp.add, [parts[k, 0:depth, :].astype(F32) for k in range(parts.shape[0])])
    tails = [parts[k, depth:deep, :].astype(F32) for k in range(parts.shape[0])]
    out[...] = (total / add_three(functools.reduce(jnp.add, tails))).astype(BF16)


def everyone(val, axes):
    count = lax.axis_size(axes)
    copies = jnp.broadcast_to(val[None], (count,) + val.shape)
    return lax.all_to_all(copies, axes, 0, 0, tiled=True)


def swapped(val):
    return lax.ppermute(val, "c", [(0, 1), (1, 0)])


def on_device(noise, data, *, vmem=in_vmem):
    zs, xs, cs, cols_all = (lax.axis_size(a) for a in ("z", "x", "c", "col"))
    half, slice_width = noise.shape
    rows = half * cs
    depth = slice_width * cols_all
    wide = data.shape[0] * zs * xs
    count_noise, count_data = float(rows * zs * xs), float(wide * cs * cols_all)
    log_data = math.log(count_data)
    row_axes, col_axes = ("z", "x"), ("col", "c")

    noise_parts = lax.all_gather(noise.T, ("col", "c"), axis=0)
    noise_parts = noise_parts.reshape(cols_all, cs, slice_width, half)
    data_all = everyone(data, ("z", "x")).reshape(wide, depth)

    vec_col = jax.ShapeDtypeStruct((wide // 128, 128), F32)
    vec_row = jax.ShapeDtypeStruct((rows // 128, 128), F32)
    tile = vmem((rows, wide), F32)
    strip = pltpu.VMEM((rows, 128), F32)

    noise_all, noise_sq = call(
        noise_body, (jax.ShapeDtypeStruct((rows, depth), BF16), vec_row), 1, name="noise"
    )(noise_parts)
    score, lse = call(
        cost_body, (tile, vec_col), 3, [strip, pltpu.VMEM((wide, 128), F32)], name="cost"
    )(noise_all, noise_sq, data_all)
    parts = everyone(lse, row_axes)
    expd, peak, lse = call(
        functools.partial(first_row_body, log_data, 1),
        (tile, vec_row, vec_row), 2, [strip, strip], name="first_rows",
    )(parts, score)
    parts = everyone(lse, col_axes)
    sums, scale = call(
        functools.partial(first_col_body, count_noise, 1),
        (vec_col, vec_row), 3, [strip], name="first_cols",
    )(parts, peak, expd)
    for sweep in range(1, ITERS - 1):
        parts = everyone(sums, row_axes)
        mass = call(
            functools.partial(row_body, count_data, 1), vec_row, 3, [strip], name="rows"
        )(parts, scale, expd)
        parts = everyone(mass, col_axes)
        last = sweep == ITERS - 2
        sums, *factor = call(
            functools.partial(col_body, count_noise, 1),
            (vec_col, vec_row) if last else (vec_col,), 3, [strip], name="cols",
        )(parts, scale, expd)
    (factor,) = factor
    parts = everyone(sums, row_axes)

    strips = [pltpu.VMEM((half, 128), F32)] * 2 + [pltpu.VMEM((half, wide), BF16)]
    packed = jax.ShapeDtypeStruct((cols_all, slice_width + 16, half), BF16)
    far = call(
        functools.partial(target_body, count_data, 1, 1), packed, 4, strips, name="targets_far"
    )(parts, factor, expd, data_all)
    far = swapped(far)
    mine, mass = call(
        functools.partial(target_body, count_data, 0, 1),
        (vmem((cols_all, slice_width, half), F32), jax.ShapeDtypeStruct((half // 128, 128), F32)),
        4, strips, name="targets_own",
    )(parts, factor, expd, data_all)
    pieces = call(pack_body, packed, 3, name="pack")(mine, mass, far)
    got = lax.all_to_all(pieces, "col", 0, 0, tiled=True)
    out = call(finish_body, jax.ShapeDtypeStruct((slice_width, half), BF16), 1, name="finish")(got)
    return out.T


def solution(mesh):
    rows, cols = mesh.devices.shape
    parts = (rows // (XS * CORES), XS, CORES, cols)
    split = jax.sharding.Mesh(mesh.devices.reshape(parts), ("z", "x", "c", "col"))
    return jax.shard_map(
        on_device,
        mesh=split,
        in_specs=(P(("z", "x", "c"), "col"), P(("col", "z", "x", "c"), None)),
        out_specs=P(("z", "x", "c"), "col"),
        check_vma=False,
    )
```

```python
import functools
import math

import jax
import jax.numpy as jnp
from jax import lax
from jax.experimental import pallas as pl
from jax.experimental.pallas import tpu as pltpu
from jax.sharding import PartitionSpec as P

ITERS = 4
EPS = 0.01
CORES, XS = 2, 4
SHIFT = 24.0 * math.log(2.0)
SCALE = 2.0**48
F32, BF16 = jnp.float32, jnp.bfloat16
VM = pl.BlockSpec(memory_space=pltpu.VMEM)


def params(mib):
    return pltpu.CompilerParams(vmem_limit_bytes=mib * 2**20)


def in_vmem(shape, dtype):
    return pltpu.VMEM(shape, dtype)


def call(body, outs, count, scratch=(), mib=32, name=None):
    return pl.pallas_call(
        body,
        out_shape=outs,
        in_specs=[VM] * count,
        out_specs=jax.tree.map(lambda _: VM, outs, is_leaf=lambda o: hasattr(o, "dtype")),
        scratch_shapes=list(scratch),
        compiler_params=params(mib),
        name=name,
    )


def lanes_to_rows(vec, out_ref):
    for r in range(vec.shape[0]):
        block = jnp.broadcast_to(vec[r : r + 1, :], (128, 128))
        out_ref[r * 128 : (r + 1) * 128, :] = block.T


def rows_to_lanes(ref):
    parts = []
    for r in range(ref.shape[0] // 128):
        parts.append(jnp.sum(ref[r * 128 : (r + 1) * 128, :].T, axis=0, keepdims=True))
    return jnp.concatenate(parts, axis=0)


def flat(vec):
    return jnp.concatenate([vec[t : t + 1, :] for t in range(vec.shape[0])], axis=1)


def lane_sum(val):
    total = val[:, 0:128]
    for t in range(1, val.shape[1] // 128):
        total = total + val[:, t * 128 : (t + 1) * 128]
    return total


def parts_of(refs):
    parts = []
    for ref in refs:
        if len(ref.shape) == 3:
            parts += [ref[k] for k in range(ref.shape[0])]
        else:
            parts.append(ref[...])
    return parts


def merged(refs):
    parts = parts_of(refs)
    top = functools.reduce(jnp.maximum, parts)
    return top + jnp.log(sum(jnp.exp(part - top) for part in parts))


def added(refs):
    return functools.reduce(jnp.add, [part.astype(F32) for part in parts_of(refs)])


def half_at(flip, rows):
    return pl.multiple_of(lax.rem(lax.axis_index("c") + flip, 2) * rows, rows)


def noise_body(parts, out):
    for r in range(out.shape[0] // 128):
        at = slice(r * 128, (r + 1) * 128)
        blocks = [parts[k, :, at].astype(F32).T for k in range(parts.shape[0])]
        out[at, :] = jnp.concatenate(blocks, axis=1).astype(BF16)


def cost_body(noise, data, *refs):
    *before, score, lse, data_sq, rows_sq, part = refs
    rows, depth = noise.shape
    width = 256
    contract = (((1,), (1,)), ((), ()))
    for r in range(rows // 128):
        block = noise[r * 128 : (r + 1) * 128, :].astype(F32)
        total = jnp.sum(lane_sum(block * block), axis=1, keepdims=True)
        rows_sq[r * 128 : (r + 1) * 128, :] = jnp.broadcast_to(total, (128, 128))
    for b in range(data.shape[0] // width):
        at = slice(b * width, (b + 1) * width)
        piece = data[at, :]
        places = slice(b * (width // 128), (b + 1) * (width // 128))
        if before:
            data_sq[places, :] = before[1][places, :]
        else:
            wide = piece.astype(F32)
            part[at, :] = lane_sum(wide * wide)
            data_sq[places, :] = rows_to_lanes(part.at[at, :])
        piece_sq = flat(data_sq[places, :])
        cross = lax.dot_general(noise[...], piece, contract, preferred_element_type=F32)
        sq = jnp.concatenate([rows_sq[...]] * (width // 128), axis=1)
        val = (2.0 * cross - sq - piece_sq) * (1.0 / (depth * EPS))
        score[:, at] = val
        top = jnp.max(val, axis=0, keepdims=True)
        total = jnp.sum(jnp.exp(val - top), axis=0, keepdims=True)
        sums = top + jnp.log(total)
        for t in range(width // 128):
            row = slice(b * (width // 128) + t, b * (width // 128) + t + 1)
            lse[row, :] = sums[:, t * 128 : (t + 1) * 128]
    if before:
        lse[...] = merged([lse, before[0]])


def first_row_body(log_data, n, *refs):
    parts, (own, far, expd, peak, lse, part, tops) = refs[:n], refs[n:]
    rows, cols = expd.shape
    half = own.shape[0]
    pot = jnp.broadcast_to(flat(-log_data - merged(parts)), (8, cols))

    def rows_at(base, r):
        return pl.ds(pl.multiple_of(base + r * 8, 8), 8)

    for flip, score in enumerate((own, far)):
        base = half_at(flip, half)

        def find(r, carry):
            val = score[rows_at(0, r), :] + pot
            part[rows_at(base, r), :] = functools.reduce(
                jnp.maximum, [val[:, t * 128 : (t + 1) * 128] for t in range(cols // 128)]
            )
            return carry

        lax.fori_loop(0, half // 8, find, 0, unroll=8)
    high = jnp.concatenate(
        [
            jnp.max(part[r * 128 : (r + 1) * 128, :].T, axis=0, keepdims=True)
            for r in range(rows // 128)
        ],
        axis=0,
    )
    lanes_to_rows(high - SHIFT, tops)
    for flip, score in enumerate((own, far)):
        base = half_at(flip, half)

        def raise_up(r, carry):
            at = rows_at(base, r)
            top = jnp.concatenate([tops[at, :]] * (cols // 128), axis=1)
            e = jnp.exp((score[rows_at(0, r), :] + pot) - top)
            expd[at, :] = e
            part[at, :] = lane_sum(e)
            return carry

        lax.fori_loop(0, half // 8, raise_up, 0, unroll=8)
    peak[...] = high
    lse[...] = high + (jnp.log(rows_to_lanes(part)) - SHIFT)


def column_sums(expd, factor, factors, out):
    lanes_to_rows(factor, factors)
    rows, cols = expd.shape
    copies = cols // 128

    def body(r, acc):
        at = pl.ds(pl.multiple_of(r * 8, 8), 8)
        f = factors[at, :]
        return acc + expd[at, :] * jnp.concatenate([f] * copies, axis=1)

    acc = lax.fori_loop(0, rows // 8, body, jnp.zeros((8, cols), F32), unroll=8)
    sums = jnp.sum(acc, axis=0, keepdims=True)
    count, width = out.shape
    rows_out = factors.at[0:count, :]
    for t in range(count):
        rows_out[t : t + 1, :] = sums[:, t * width : (t + 1) * width]
    out[...] = rows_out[...].astype(out.dtype)


def first_col_body(count, n, *refs):
    parts, (peak, expd, out, scale, factors) = refs[:n], refs[n:]
    s = jnp.exp(peak[...] - merged(parts) + SHIFT)
    scale[...] = s
    column_sums(expd, s * (1.0 / count), factors, out)


def col_body(count, n, *refs):
    parts, (scale, expd, out, *factor, factors) = refs[:n], refs[n:]
    f = scale[...] * ((SCALE / count) / added(parts))
    for ref in factor:
        ref[...] = f
    column_sums(expd, f, factors, out)


def row_body(count, n, *refs):
    parts, (scale, expd, out, part) = refs[:n], refs[n:]
    v = jnp.broadcast_to(flat((SCALE / count) / added(parts)), (8, expd.shape[1]))
    rows = expd.shape[0]

    def body(r, carry):
        at = pl.ds(pl.multiple_of(r * 8, 8), 8)
        part[at, :] = lane_sum(expd[at, :] * v)
        return carry

    lax.fori_loop(0, rows // 8, body, 0, unroll=8)
    out[...] = (rows_to_lanes(part) * scale[...]).astype(out.dtype)


def split_three(mass, deep):
    high = mass.astype(BF16).astype(F32)
    mid = (mass - high).astype(BF16).astype(F32)
    zero = jnp.zeros((deep - 3, mass.shape[1]), F32)
    return jnp.concatenate([high, mid, mass - high - mid, zero], axis=0)


def add_three(tail):
    return tail[0:1, :] + tail[1:2, :] + tail[2:3, :]


def target_body(count, flip, n, *refs):
    parts, (factor, expd, data, out) = refs[:n], refs[n : n + 4]
    *mass, part, factors = refs[n + 4 :]
    v = jnp.broadcast_to(flat((SCALE / count) / added(parts)), (128, expd.shape[1]))
    half, wide = factors.shape[0], expd.shape[1]
    base = half_at(flip, half)
    first = lax.rem(lax.axis_index("c") + flip, 2) * (half // 128)
    lanes_to_rows(factor[pl.ds(first, half // 128), :], factors)
    cols, deep, _ = out.shape
    depth = data.shape[1] // cols
    for r in range(half // 128):
        at = slice(r * 128, (r + 1) * 128)
        f = jnp.concatenate([factors[at, :]] * (wide // 128), axis=1)
        w = expd[pl.ds(pl.multiple_of(base + r * 128, 128), 128), :] * v * f
        total = jnp.sum(lane_sum(w).T, axis=0, keepdims=True)
        part[r : r + 1, :] = total
        block = jnp.dot(w.astype(BF16), data[...], preferred_element_type=F32).T
        tail = [] if mass else [split_three(total, deep - depth)]
        for k in range(cols):
            rows = [block[k * depth : (k + 1) * depth, :]] + tail
            out[k, :, at] = jnp.concatenate(rows, axis=0).astype(out.dtype)
    for ref in mass:
        ref[...] = part[...]


def pack_body(own, mass, far, out):
    depth, deep = own.shape[1], out.shape[1]
    parts = [far[k].astype(F32) for k in range(out.shape[0])]
    tail = split_three(flat(mass[...]) + add_three(parts[0][depth:deep, :]), deep - depth)
    for k, part in enumerate(parts):
        out[k] = jnp.concatenate([own[k] + part[0:depth, :], tail], axis=0).astype(BF16)


def finish_body(parts, out):
    depth = out.shape[0]
    total = functools.reduce(jnp.add, [parts[k].astype(F32) for k in range(parts.shape[0])])
    out[...] = (total[0:depth, :] / add_three(total[depth:, :])).astype(BF16)


def spread_body(val, out):
    for k in range(out.shape[0]):
        out[k] = val[...]


def everyone(val, axes):
    count = lax.axis_size(axes)
    copies = jnp.broadcast_to(val[None], (count,) + val.shape)
    return lax.all_to_all(copies, axes, 0, 0, tiled=True)


def swapped(val):
    return lax.ppermute(val, "c", [(0, 1), (1, 0)])


def on_device(noise, data, *, vmem=in_vmem):
    zs, xs, cs, cols_all = (lax.axis_size(a) for a in ("z", "x", "c", "col"))
    half, slice_width = noise.shape
    rows = half * cs
    depth = slice_width * cols_all
    wide = data.shape[0] * zs * xs
    count_noise, count_data = float(rows * zs * xs), float(wide * cs * cols_all)
    log_data = math.log(count_data)
    row_axes, col_axes = ("z", "x"), ("col", "c")

    noise_parts = lax.all_gather(noise.T, "col", axis=0)
    copies = call(spread_body, vmem((zs * xs,) + data.shape, BF16), 1, name="spread")(data)
    data_all = lax.all_to_all(copies, row_axes, 0, 0, tiled=True).reshape(wide, depth)
    own = call(noise_body, jax.ShapeDtypeStruct((half, depth), BF16), 1, name="noise")(noise_parts)
    far = swapped(own)

    vec_col = jax.ShapeDtypeStruct((wide // 128, 128), F32)
    sent_col = jax.ShapeDtypeStruct((wide // 128, 128), BF16)
    sent_row = jax.ShapeDtypeStruct((rows // 128, 128), BF16)
    vec_row = jax.ShapeDtypeStruct((rows // 128, 128), F32)
    strip = pltpu.VMEM((rows, 128), F32)

    cost_outs = (vmem((half, wide), F32), vec_col, vec_col)
    cost_scratch = [pltpu.VMEM((half, 128), F32), pltpu.VMEM((wide, 128), F32)]
    score_own, *before = call(cost_body, cost_outs, 2, cost_scratch, name="cost_own")(own, data_all)
    score_far, lse, _ = call(cost_body, cost_outs, 4, cost_scratch, name="cost_far")(far, data_all, *before)
    parts = everyone(lse, row_axes)
    expd, peak, lse = call(
        functools.partial(first_row_body, log_data, 1),
        (vmem((rows, wide), F32), vec_row, vec_row), 3, [strip, strip], name="first_rows",
    )(parts, score_own, score_far)
    parts = everyone(lse, col_axes)
    sums, scale = call(
        functools.partial(first_col_body, count_noise, 1),
        (sent_col, vec_row), 3, [strip], name="first_cols",
    )(parts, peak, expd)
    for sweep in range(1, ITERS - 1):
        parts = everyone(sums, row_axes)
        mass = call(
            functools.partial(row_body, count_data, 1), sent_row, 3, [strip], name="rows"
        )(parts, scale, expd)
        parts = everyone(mass, col_axes)
        last = sweep == ITERS - 2
        sums, *factor = call(
            functools.partial(col_body, count_noise, 1),
            (sent_col, vec_row) if last else (sent_col,), 3, [strip], name="cols",
        )(parts, scale, expd)
    (factor,) = factor
    parts = everyone(sums, row_axes)

    strips = [pltpu.VMEM((half // 128, 128), F32), pltpu.VMEM((half, 128), F32)]
    packed = jax.ShapeDtypeStruct((cols_all, slice_width + 8, half), BF16)
    far = call(
        functools.partial(target_body, count_data, 1, 1), packed, 4, strips, name="targets_far"
    )(parts, factor, expd, data_all)
    far = swapped(far)
    mine, mass = call(
        functools.partial(target_body, count_data, 0, 1),
        (vmem((cols_all, slice_width, half), F32), jax.ShapeDtypeStruct((half // 128, 128), F32)),
        4, strips, name="targets_own",
    )(parts, factor, expd, data_all)
    pieces = call(pack_body, packed, 3, name="pack")(mine, mass, far)
    got = lax.all_to_all(pieces, "col", 0, 0, tiled=True)
    out = call(finish_body, jax.ShapeDtypeStruct((slice_width, half), BF16), 1, name="finish")(got)
    return out.T


def solution(mesh):
    rows, cols = mesh.devices.shape
    parts = (rows // (XS * CORES), XS, CORES, cols)
    split = jax.sharding.Mesh(mesh.devices.reshape(parts), ("z", "x", "c", "col"))
    return jax.shard_map(
        on_device,
        mesh=split,
        in_specs=(P(("z", "x", "c"), "col"), P(("col", "z", "x", "c"), None)),
        out_specs=P(("z", "x", "c"), "col"),
        check_vma=False,
    )
```

```python
import functools
import math

import jax
import jax.numpy as jnp
from jax import lax
from jax.experimental import pallas as pl
from jax.experimental.pallas import tpu as pltpu
from jax.sharding import PartitionSpec as P

ITERS = 4
EPS = 0.01
CORES, XS = 2, 4
SHIFT = 24.0
SCALE = 2.0**48
F32, BF16 = jnp.float32, jnp.bfloat16
VM = pl.BlockSpec(memory_space=pltpu.VMEM)


def params(mib):
    return pltpu.CompilerParams(vmem_limit_bytes=mib * 2**20)


def in_vmem(shape, dtype):
    return pltpu.VMEM(shape, dtype)


def call(body, outs, count, scratch=(), mib=32, name=None):
    return pl.pallas_call(
        body,
        out_shape=outs,
        in_specs=[VM] * count,
        out_specs=jax.tree.map(lambda _: VM, outs, is_leaf=lambda o: hasattr(o, "dtype")),
        scratch_shapes=list(scratch),
        compiler_params=params(mib),
        name=name,
    )


def lanes_to_rows(vec, out_ref):
    for r in range(vec.shape[0]):
        block = jnp.broadcast_to(vec[r : r + 1, :], (128, 128))
        out_ref[r * 128 : (r + 1) * 128, :] = block.T


def rows_to_lanes(ref):
    parts = []
    for r in range(ref.shape[0] // 128):
        parts.append(jnp.sum(ref[r * 128 : (r + 1) * 128, :].T, axis=0, keepdims=True))
    return jnp.concatenate(parts, axis=0)


def flat(vec):
    return jnp.concatenate([vec[t : t + 1, :] for t in range(vec.shape[0])], axis=1)


def lane_sum(val):
    total = val[:, 0:128]
    for t in range(1, val.shape[1] // 128):
        total = total + val[:, t * 128 : (t + 1) * 128]
    return total


def parts_of(refs):
    parts = []
    for ref in refs:
        if len(ref.shape) == 3:
            parts += [ref[k] for k in range(ref.shape[0])]
        else:
            parts.append(ref[...])
    return parts


def merged(refs):
    parts = parts_of(refs)
    top = functools.reduce(jnp.maximum, parts)
    return top + jnp.log2(sum(jnp.exp2(part - top) for part in parts))


def added(refs):
    return functools.reduce(jnp.add, [part.astype(F32) for part in parts_of(refs)])


def half_at(flip, rows):
    return pl.multiple_of(lax.rem(lax.axis_index("c") + flip, 2) * rows, rows)


def noise_body(parts, out):
    for r in range(out.shape[0] // 128):
        at = slice(r * 128, (r + 1) * 128)
        blocks = [parts[k, :, at].astype(F32).T for k in range(parts.shape[0])]
        out[at, :] = jnp.concatenate(blocks, axis=1).astype(BF16)


def cost_body(noise, data, *refs):
    *before, score, lse, data_sq, rows_sq, part = refs
    rows, depth = noise.shape
    width = 256
    factor = math.log2(math.e) / (depth * EPS)
    contract = (((1,), (1,)), ((), ()))
    for r in range(rows // 128):
        block = noise[r * 128 : (r + 1) * 128, :].astype(F32)
        total = jnp.sum(lane_sum(block * block), axis=1, keepdims=True)
        rows_sq[r * 128 : (r + 1) * 128, :] = jnp.broadcast_to(total * factor, (128, 128))
    for b in range(data.shape[0] // width):
        at = slice(b * width, (b + 1) * width)
        piece = data[at, :]
        places = slice(b * (width // 128), (b + 1) * (width // 128))
        if before:
            data_sq[places, :] = before[1][places, :]
        else:
            wide = piece.astype(F32)
            part[at, :] = lane_sum(wide * wide)
            data_sq[places, :] = rows_to_lanes(part.at[at, :]) * factor
        piece_sq = flat(data_sq[places, :])
        cross = lax.dot_general(noise[...], piece, contract, preferred_element_type=F32)
        sq = jnp.concatenate([rows_sq[...]] * (width // 128), axis=1)
        val = cross * (2.0 * factor) - sq - piece_sq
        score[:, at] = val
        top = jnp.max(val, axis=0, keepdims=True)
        total = jnp.sum(jnp.exp2(val - top), axis=0, keepdims=True)
        sums = top + jnp.log2(total)
        for t in range(width // 128):
            row = slice(b * (width // 128) + t, b * (width // 128) + t + 1)
            lse[row, :] = sums[:, t * 128 : (t + 1) * 128]
    if before:
        lse[...] = merged([lse, before[0]])


def first_row_body(log_data, n, *refs):
    parts, (own, far, expd, peak, lse, part, tops) = refs[:n], refs[n:]
    rows, cols = expd.shape
    half = own.shape[0]
    pot = jnp.broadcast_to(flat(-log_data - merged(parts)), (8, cols))

    def rows_at(base, r):
        return pl.ds(pl.multiple_of(base + r * 8, 8), 8)

    for flip, score in enumerate((own, far)):
        base = half_at(flip, half)

        def find(r, carry):
            val = score[rows_at(0, r), :] + pot
            part[rows_at(base, r), :] = functools.reduce(
                jnp.maximum, [val[:, t * 128 : (t + 1) * 128] for t in range(cols // 128)]
            )
            return carry

        lax.fori_loop(0, half // 8, find, 0, unroll=8)
    high = jnp.concatenate(
        [
            jnp.max(part[r * 128 : (r + 1) * 128, :].T, axis=0, keepdims=True)
            for r in range(rows // 128)
        ],
        axis=0,
    )
    lanes_to_rows(high - SHIFT, tops)
    for flip, score in enumerate((own, far)):
        base = half_at(flip, half)

        def raise_up(r, carry):
            at = rows_at(base, r)
            top = jnp.concatenate([tops[at, :]] * (cols // 128), axis=1)
            e = jnp.exp2((score[rows_at(0, r), :] + pot) - top)
            expd[at, :] = e
            part[at, :] = lane_sum(e)
            return carry

        lax.fori_loop(0, half // 8, raise_up, 0, unroll=8)
    peak[...] = high
    lse[...] = high + (jnp.log2(rows_to_lanes(part)) - SHIFT)


def column_sums(expd, factor, factors, out):
    lanes_to_rows(factor, factors)
    rows, cols = expd.shape
    copies = cols // 128

    def body(r, acc):
        at = pl.ds(pl.multiple_of(r * 8, 8), 8)
        f = factors[at, :]
        return acc + expd[at, :] * jnp.concatenate([f] * copies, axis=1)

    acc = lax.fori_loop(0, rows // 8, body, jnp.zeros((8, cols), F32), unroll=8)
    sums = jnp.sum(acc, axis=0, keepdims=True)
    count, width = out.shape
    rows_out = factors.at[0:count, :]
    for t in range(count):
        rows_out[t : t + 1, :] = sums[:, t * width : (t + 1) * width]
    out[...] = rows_out[...].astype(out.dtype)


def first_col_body(count, n, *refs):
    parts, (peak, expd, out, scale, factors) = refs[:n], refs[n:]
    s = jnp.exp2(peak[...] - merged(parts) + SHIFT)
    scale[...] = s
    column_sums(expd, s * (1.0 / count), factors, out)


def col_body(count, n, *refs):
    parts, (scale, expd, out, *factor, factors) = refs[:n], refs[n:]
    f = scale[...] * ((SCALE / count) / added(parts))
    for ref in factor:
        ref[...] = f
    column_sums(expd, f, factors, out)


def row_body(count, n, *refs):
    parts, (scale, expd, out, part) = refs[:n], refs[n:]
    v = jnp.broadcast_to(flat((SCALE / count) / added(parts)), (8, expd.shape[1]))
    rows = expd.shape[0]

    def body(r, carry):
        at = pl.ds(pl.multiple_of(r * 8, 8), 8)
        part[at, :] = lane_sum(expd[at, :] * v)
        return carry

    lax.fori_loop(0, rows // 8, body, 0, unroll=8)
    out[...] = (rows_to_lanes(part) * scale[...]).astype(out.dtype)


def split_three(mass, deep):
    high = mass.astype(BF16).astype(F32)
    mid = (mass - high).astype(BF16).astype(F32)
    zero = jnp.zeros((deep - 3, mass.shape[1]), F32)
    return jnp.concatenate([high, mid, mass - high - mid, zero], axis=0)


def add_three(tail):
    return tail[0:1, :] + tail[1:2, :] + tail[2:3, :]


def target_body(count, flip, n, *refs):
    parts, (factor, expd, data, out) = refs[:n], refs[n : n + 4]
    *mass, part, factors = refs[n + 4 :]
    v = jnp.broadcast_to(flat((SCALE / count) / added(parts)), (128, expd.shape[1]))
    half, wide = factors.shape[0], expd.shape[1]
    base = half_at(flip, half)
    first = lax.rem(lax.axis_index("c") + flip, 2) * (half // 128)
    lanes_to_rows(factor[pl.ds(first, half // 128), :], factors)
    cols, deep, _ = out.shape
    depth = data.shape[1] // cols
    for r in range(half // 128):
        at = slice(r * 128, (r + 1) * 128)
        f = jnp.concatenate([factors[at, :]] * (wide // 128), axis=1)
        w = expd[pl.ds(pl.multiple_of(base + r * 128, 128), 128), :] * v * f
        total = jnp.sum(lane_sum(w).T, axis=0, keepdims=True)
        part[r : r + 1, :] = total
        block = jnp.dot(w.astype(BF16), data[...], preferred_element_type=F32).T
        tail = [] if mass else [split_three(total, deep - depth)]
        for k in range(cols):
            rows = [block[k * depth : (k + 1) * depth, :]] + tail
            out[k, :, at] = jnp.concatenate(rows, axis=0).astype(out.dtype)
    for ref in mass:
        ref[...] = part[...]


def pack_body(own, mass, far, out):
    depth, deep = own.shape[1], out.shape[1]
    parts = [far[k].astype(F32) for k in range(out.shape[0])]
    tail = split_three(flat(mass[...]) + add_three(parts[0][depth:deep, :]), deep - depth)
    for k, part in enumerate(parts):
        out[k] = jnp.concatenate([own[k] + part[0:depth, :], tail], axis=0).astype(BF16)


def finish_body(parts, out):
    depth = out.shape[0]
    total = functools.reduce(jnp.add, [parts[k].astype(F32) for k in range(parts.shape[0])])
    out[...] = (total[0:depth, :] / add_three(total[depth:, :])).astype(BF16)


def spread_body(val, out, held, sem_in, sems):
    come = pltpu.make_async_copy(val, held, sem_in)
    come.start()
    come.wait()
    copies = [pltpu.make_async_copy(held, out.at[k], sems.at[k]) for k in range(out.shape[0])]
    for copy in copies:
        copy.start()
    for copy in copies:
        copy.wait()


def spread(val, count):
    whole = pl.BlockSpec(memory_space=pl.ANY)
    return pl.pallas_call(
        spread_body,
        out_shape=jax.ShapeDtypeStruct((count,) + val.shape, val.dtype),
        in_specs=[whole],
        out_specs=whole,
        scratch_shapes=[
            pltpu.VMEM(val.shape, val.dtype),
            pltpu.SemaphoreType.DMA,
            pltpu.SemaphoreType.DMA((count,)),
        ],
        compiler_params=params(32),
        name="spread",
    )(val)


def everyone(val, axes):
    count = lax.axis_size(axes)
    copies = jnp.broadcast_to(val[None], (count,) + val.shape)
    return lax.all_to_all(copies, axes, 0, 0, tiled=True)


def swapped(val):
    return lax.ppermute(val, "c", [(0, 1), (1, 0)])


def on_device(noise, data, *, vmem=in_vmem):
    zs, xs, cs, cols_all = (lax.axis_size(a) for a in ("z", "x", "c", "col"))
    half, slice_width = noise.shape
    rows = half * cs
    depth = slice_width * cols_all
    wide = data.shape[0] * zs * xs
    count_noise, count_data = float(rows * zs * xs), float(wide * cs * cols_all)
    log_data = math.log2(count_data)
    row_axes, col_axes = ("z", "x"), ("col", "c")

    noise_parts = lax.all_gather(noise.T, "col", axis=0)
    copies = spread(data, zs * xs)
    data_all = lax.all_to_all(copies, row_axes, 0, 0, tiled=True).reshape(wide, depth)
    own = call(noise_body, jax.ShapeDtypeStruct((half, depth), BF16), 1, name="noise")(noise_parts)
    far = swapped(own)

    vec_col = jax.ShapeDtypeStruct((wide // 128, 128), F32)
    sent_col = jax.ShapeDtypeStruct((wide // 128, 128), BF16)
    sent_row = jax.ShapeDtypeStruct((rows // 128, 128), BF16)
    vec_row = jax.ShapeDtypeStruct((rows // 128, 128), F32)
    strip = pltpu.VMEM((rows, 128), F32)

    cost_outs = (vmem((half, wide), F32), vec_col, vec_col)
    cost_scratch = [pltpu.VMEM((half, 128), F32), pltpu.VMEM((wide, 128), F32)]
    score_own, *before = call(cost_body, cost_outs, 2, cost_scratch, name="cost_own")(own, data_all)
    score_far, lse, _ = call(cost_body, cost_outs, 4, cost_scratch, name="cost_far")(far, data_all, *before)
    parts = everyone(lse, row_axes)
    expd, peak, lse = call(
        functools.partial(first_row_body, log_data, 1),
        (vmem((rows, wide), F32), vec_row, vec_row), 3, [strip, strip], name="first_rows",
    )(parts, score_own, score_far)
    parts = everyone(lse, col_axes)
    sums, scale = call(
        functools.partial(first_col_body, count_noise, 1),
        (sent_col, vec_row), 3, [strip], name="first_cols",
    )(parts, peak, expd)
    for sweep in range(1, ITERS - 1):
        parts = everyone(sums, row_axes)
        mass = call(
            functools.partial(row_body, count_data, 1), sent_row, 3, [strip], name="rows"
        )(parts, scale, expd)
        parts = everyone(mass, col_axes)
        last = sweep == ITERS - 2
        sums, *factor = call(
            functools.partial(col_body, count_noise, 1),
            (sent_col, vec_row) if last else (sent_col,), 3, [strip], name="cols",
        )(parts, scale, expd)
    (factor,) = factor
    parts = everyone(sums, row_axes)

    strips = [pltpu.VMEM((half // 128, 128), F32), pltpu.VMEM((half, 128), F32)]
    packed = jax.ShapeDtypeStruct((cols_all, slice_width + 8, half), BF16)
    far = call(
        functools.partial(target_body, count_data, 1, 1), packed, 4, strips, name="targets_far"
    )(parts, factor, expd, data_all)
    far = swapped(far)
    mine, mass = call(
        functools.partial(target_body, count_data, 0, 1),
        (vmem((cols_all, slice_width, half), F32), jax.ShapeDtypeStruct((half // 128, 128), F32)),
        4, strips, name="targets_own",
    )(parts, factor, expd, data_all)
    pieces = call(pack_body, packed, 3, name="pack")(mine, mass, far)
    got = lax.all_to_all(pieces, "col", 0, 0, tiled=True)
    out = call(finish_body, jax.ShapeDtypeStruct((slice_width, half), BF16), 1, name="finish")(got)
    return out.T


def solution(mesh):
    rows, cols = mesh.devices.shape
    parts = (rows // (XS * CORES), XS, CORES, cols)
    split = jax.sharding.Mesh(mesh.devices.reshape(parts), ("z", "x", "c", "col"))
    return jax.shard_map(
        on_device,
        mesh=split,
        in_specs=(P(("z", "x", "c"), "col"), P(("col", "z", "x", "c"), None)),
        out_specs=P(("z", "x", "c"), "col"),
        check_vma=False,
    )
```

```python
import functools
import math

import jax
import jax.numpy as jnp
from jax import lax
from jax.experimental import pallas as pl
from jax.experimental.pallas import tpu as pltpu
from jax.sharding import PartitionSpec as P

ITERS = 4
EPS = 0.01
CORES, XS = 2, 4
COL = ("yh", "yl")
SHIFT = 24.0
SCALE = 2.0**48
F32, BF16 = jnp.float32, jnp.bfloat16
VM = pl.BlockSpec(memory_space=pltpu.VMEM)


def params(mib):
    return pltpu.CompilerParams(vmem_limit_bytes=mib * 2**20)


def in_vmem(shape, dtype):
    return pltpu.VMEM(shape, dtype)


def call(body, outs, count, scratch=(), mib=32, name=None):
    return pl.pallas_call(
        body,
        out_shape=outs,
        in_specs=[VM] * count,
        out_specs=jax.tree.map(lambda _: VM, outs, is_leaf=lambda o: hasattr(o, "dtype")),
        scratch_shapes=list(scratch),
        compiler_params=params(mib),
        name=name,
    )


def lanes_to_rows(vec, out_ref):
    for r in range(vec.shape[0]):
        block = jnp.broadcast_to(vec[r : r + 1, :], (128, 128))
        out_ref[r * 128 : (r + 1) * 128, :] = block.T


def rows_to_lanes(ref):
    parts = []
    for r in range(ref.shape[0] // 128):
        parts.append(jnp.sum(ref[r * 128 : (r + 1) * 128, :].T, axis=0, keepdims=True))
    return jnp.concatenate(parts, axis=0)


def flat(vec):
    return jnp.concatenate([vec[t : t + 1, :] for t in range(vec.shape[0])], axis=1)


def lane_sum(val):
    total = val[:, 0:128]
    for t in range(1, val.shape[1] // 128):
        total = total + val[:, t * 128 : (t + 1) * 128]
    return total


def parts_of(refs):
    parts = []
    for ref in refs:
        if len(ref.shape) == 3:
            parts += [ref[k] for k in range(ref.shape[0])]
        else:
            parts.append(ref[...])
    return parts


def merged(refs):
    parts = parts_of(refs)
    top = functools.reduce(jnp.maximum, parts)
    return top + jnp.log2(sum(jnp.exp2(part - top) for part in parts))


def added(refs):
    return functools.reduce(jnp.add, [part.astype(F32) for part in parts_of(refs)])


def half_at(flip, rows):
    return pl.multiple_of(lax.rem(lax.axis_index("c") + flip, 2) * rows, rows)


def noise_body(parts, out):
    for r in range(out.shape[0] // 128):
        at = slice(r * 128, (r + 1) * 128)
        blocks = [parts[k, :, at].astype(F32).T for k in range(parts.shape[0])]
        out[at, :] = jnp.concatenate(blocks, axis=1).astype(BF16)


def cost_body(noise, data, *refs):
    *before, score, lse, data_sq, rows_sq, part = refs
    rows, depth = noise.shape
    width = 256
    factor = math.log2(math.e) / (depth * EPS)
    contract = (((1,), (1,)), ((), ()))
    for r in range(rows // 128):
        block = noise[r * 128 : (r + 1) * 128, :].astype(F32)
        total = jnp.sum(lane_sum(block * block), axis=1, keepdims=True)
        rows_sq[r * 128 : (r + 1) * 128, :] = jnp.broadcast_to(total * factor, (128, 128))
    for b in range(data.shape[0] // width):
        at = slice(b * width, (b + 1) * width)
        piece = data[at, :]
        places = slice(b * (width // 128), (b + 1) * (width // 128))
        if before:
            data_sq[places, :] = before[1][places, :]
        else:
            wide = piece.astype(F32)
            part[at, :] = lane_sum(wide * wide)
            data_sq[places, :] = rows_to_lanes(part.at[at, :]) * factor
        piece_sq = flat(data_sq[places, :])
        cross = lax.dot_general(noise[...], piece, contract, preferred_element_type=F32)
        sq = jnp.concatenate([rows_sq[...]] * (width // 128), axis=1)
        val = cross * (2.0 * factor) - sq - piece_sq
        score[:, at] = val
        top = jnp.max(val, axis=0, keepdims=True)
        total = jnp.sum(jnp.exp2(val - top), axis=0, keepdims=True)
        sums = top + jnp.log2(total)
        for t in range(width // 128):
            row = slice(b * (width // 128) + t, b * (width // 128) + t + 1)
            lse[row, :] = sums[:, t * 128 : (t + 1) * 128]
    if before:
        lse[...] = merged([lse, before[0]])


def first_row_body(log_data, n, *refs):
    parts, (own, far, expd, peak, lse, part, tops) = refs[:n], refs[n:]
    rows, cols = expd.shape
    half = own.shape[0]
    pot = jnp.broadcast_to(flat(-log_data - merged(parts)), (8, cols))

    def rows_at(base, r):
        return pl.ds(pl.multiple_of(base + r * 8, 8), 8)

    for flip, score in enumerate((own, far)):
        base = half_at(flip, half)

        def find(r, carry):
            val = score[rows_at(0, r), :] + pot
            part[rows_at(base, r), :] = functools.reduce(
                jnp.maximum, [val[:, t * 128 : (t + 1) * 128] for t in range(cols // 128)]
            )
            return carry

        lax.fori_loop(0, half // 8, find, 0, unroll=8)
    high = jnp.concatenate(
        [
            jnp.max(part[r * 128 : (r + 1) * 128, :].T, axis=0, keepdims=True)
            for r in range(rows // 128)
        ],
        axis=0,
    )
    lanes_to_rows(high - SHIFT, tops)
    for flip, score in enumerate((own, far)):
        base = half_at(flip, half)

        def raise_up(r, carry):
            at = rows_at(base, r)
            top = jnp.concatenate([tops[at, :]] * (cols // 128), axis=1)
            e = jnp.exp2((score[rows_at(0, r), :] + pot) - top)
            expd[at, :] = e
            part[at, :] = lane_sum(e)
            return carry

        lax.fori_loop(0, half // 8, raise_up, 0, unroll=8)
    peak[...] = high
    lse[...] = high + (jnp.log2(rows_to_lanes(part)) - SHIFT)


def column_sums(expd, factor, factors, out):
    lanes_to_rows(factor, factors)
    rows, cols = expd.shape
    copies = cols // 128

    def body(r, acc):
        at = pl.ds(pl.multiple_of(r * 8, 8), 8)
        f = factors[at, :]
        return acc + expd[at, :] * jnp.concatenate([f] * copies, axis=1)

    acc = lax.fori_loop(0, rows // 8, body, jnp.zeros((8, cols), F32), unroll=8)
    sums = jnp.sum(acc, axis=0, keepdims=True)
    count, width = out.shape
    rows_out = factors.at[0:count, :]
    for t in range(count):
        rows_out[t : t + 1, :] = sums[:, t * width : (t + 1) * width]
    out[...] = rows_out[...].astype(out.dtype)


def first_col_body(count, n, *refs):
    parts, (peak, expd, out, scale, factors) = refs[:n], refs[n:]
    s = jnp.exp2(peak[...] - merged(parts) + SHIFT)
    scale[...] = s
    column_sums(expd, s * (1.0 / count), factors, out)


def col_body(count, n, *refs):
    parts, (scale, expd, out, *factor, factors) = refs[:n], refs[n:]
    f = scale[...] * ((SCALE / count) / added(parts))
    for ref in factor:
        ref[...] = f
    column_sums(expd, f, factors, out)


def row_body(count, n, *refs):
    parts, (scale, expd, out, part) = refs[:n], refs[n:]
    v = jnp.broadcast_to(flat((SCALE / count) / added(parts)), (8, expd.shape[1]))
    rows = expd.shape[0]

    def body(r, carry):
        at = pl.ds(pl.multiple_of(r * 8, 8), 8)
        part[at, :] = lane_sum(expd[at, :] * v)
        return carry

    lax.fori_loop(0, rows // 8, body, 0, unroll=8)
    out[...] = (rows_to_lanes(part) * scale[...]).astype(out.dtype)


def split_three(mass, deep):
    high = mass.astype(BF16).astype(F32)
    mid = (mass - high).astype(BF16).astype(F32)
    zero = jnp.zeros((deep - 3, mass.shape[1]), F32)
    return jnp.concatenate([high, mid, mass - high - mid, zero], axis=0)


def add_three(tail):
    return tail[0:1, :] + tail[1:2, :] + tail[2:3, :]


def target_body(count, flip, n, *refs):
    parts, (factor, expd, data, out) = refs[:n], refs[n : n + 4]
    *mass, part, factors = refs[n + 4 :]
    v = jnp.broadcast_to(flat((SCALE / count) / added(parts)), (128, expd.shape[1]))
    half, wide = factors.shape[0], expd.shape[1]
    base = half_at(flip, half)
    first = lax.rem(lax.axis_index("c") + flip, 2) * (half // 128)
    lanes_to_rows(factor[pl.ds(first, half // 128), :], factors)
    cols, deep, _ = out.shape
    depth = data.shape[1] // cols
    for r in range(half // 128):
        at = slice(r * 128, (r + 1) * 128)
        f = jnp.concatenate([factors[at, :]] * (wide // 128), axis=1)
        w = expd[pl.ds(pl.multiple_of(base + r * 128, 128), 128), :] * v * f
        total = jnp.sum(lane_sum(w).T, axis=0, keepdims=True)
        part[r : r + 1, :] = total
        block = jnp.dot(w.astype(BF16), data[...], preferred_element_type=F32).T
        tail = [] if mass else [split_three(total, deep - depth)]
        for k in range(cols):
            rows = [block[k * depth : (k + 1) * depth, :]] + tail
            out[k, :, at] = jnp.concatenate(rows, axis=0).astype(out.dtype)
    for ref in mass:
        ref[...] = part[...]


def pack_body(own, mass, far, out):
    depth, deep = own.shape[1], out.shape[1]
    parts = [far[k].astype(F32) for k in range(out.shape[0])]
    tail = split_three(flat(mass[...]) + add_three(parts[0][depth:deep, :]), deep - depth)
    for k, part in enumerate(parts):
        out[k] = jnp.concatenate([own[k] + part[0:depth, :], tail], axis=0).astype(BF16)


def finish_body(parts, out):
    depth = out.shape[0]
    total = functools.reduce(jnp.add, [parts[k].astype(F32) for k in range(parts.shape[0])])
    out[...] = (total[0:depth, :] / add_three(total[depth:, :])).astype(BF16)


def pair_body(here, there, out):
    place = lax.axis_index("yl")
    out[place] = here[...]
    out[1 - place] = there[...]


def spread_body(val, out, sems):
    copies = [pltpu.make_async_copy(val, out.at[k], sems.at[k]) for k in range(out.shape[0])]
    for copy in copies:
        copy.start()
    for copy in copies:
        copy.wait()


def spread(val, count):
    return pl.pallas_call(
        spread_body,
        out_shape=jax.ShapeDtypeStruct((count,) + val.shape, val.dtype),
        in_specs=[VM],
        out_specs=pl.BlockSpec(memory_space=pl.ANY),
        scratch_shapes=[pltpu.SemaphoreType.DMA((count,))],
        compiler_params=params(32),
        name="spread",
    )(val)


def everyone(val, axes):
    count = lax.axis_size(axes)
    copies = jnp.broadcast_to(val[None], (count,) + val.shape)
    return lax.all_to_all(copies, axes, 0, 0, tiled=True)


def swapped(val, axis="c"):
    return lax.ppermute(val, axis, [(0, 1), (1, 0)])


def on_device(noise, data, *, vmem=in_vmem):
    zs, xs, cs, cols_all = (lax.axis_size(a) for a in ("z", "x", "c", COL))
    half, slice_width = noise.shape
    rows = half * cs
    depth = slice_width * cols_all
    wide = data.shape[0] * zs * xs
    count_noise, count_data = float(rows * zs * xs), float(wide * cs * cols_all)
    log_data = math.log2(count_data)
    row_axes, col_axes = ("z", "x"), COL + ("c",)

    here = noise.T
    pair = call(pair_body, jax.ShapeDtypeStruct((2,) + here.shape, BF16), 2, name="pair")(here, swapped(here, "yl"))
    noise_parts = lax.all_gather(pair, "yh", axis=0).reshape(cols_all, slice_width, half)
    copies = spread(data, zs * xs)
    data_all = lax.all_to_all(copies, row_axes, 0, 0, tiled=True).reshape(wide, depth)
    own = call(noise_body, jax.ShapeDtypeStruct((half, depth), BF16), 1, name="noise")(noise_parts)
    far = swapped(own)

    vec_col = jax.ShapeDtypeStruct((wide // 128, 128), F32)
    sent_col = jax.ShapeDtypeStruct((wide // 128, 128), BF16)
    sent_row = jax.ShapeDtypeStruct((rows // 128, 128), BF16)
    vec_row = jax.ShapeDtypeStruct((rows // 128, 128), F32)
    strip = pltpu.VMEM((rows, 128), F32)

    cost_outs = (vmem((half, wide), F32), vec_col, vec_col)
    cost_scratch = [pltpu.VMEM((half, 128), F32), pltpu.VMEM((wide, 128), F32)]
    score_own, *before = call(cost_body, cost_outs, 2, cost_scratch, name="cost_own")(own, data_all)
    score_far, lse, _ = call(cost_body, cost_outs, 4, cost_scratch, name="cost_far")(far, data_all, *before)
    parts = everyone(lse, row_axes)
    expd, peak, lse = call(
        functools.partial(first_row_body, log_data, 1),
        (vmem((rows, wide), F32), vec_row, vec_row), 3, [strip, strip], name="first_rows",
    )(parts, score_own, score_far)
    parts = everyone(lse, col_axes)
    sums, scale = call(
        functools.partial(first_col_body, count_noise, 1),
        (sent_col, vec_row), 3, [strip], name="first_cols",
    )(parts, peak, expd)
    for sweep in range(1, ITERS - 1):
        parts = everyone(sums, row_axes)
        mass = call(
            functools.partial(row_body, count_data, 1), sent_row, 3, [strip], name="rows"
        )(parts, scale, expd)
        parts = everyone(mass, col_axes)
        last = sweep == ITERS - 2
        sums, *factor = call(
            functools.partial(col_body, count_noise, 1),
            (sent_col, vec_row) if last else (sent_col,), 3, [strip], name="cols",
        )(parts, scale, expd)
    (factor,) = factor
    parts = everyone(sums, row_axes)

    strips = [pltpu.VMEM((half // 128, 128), F32), pltpu.VMEM((half, 128), F32)]
    packed = jax.ShapeDtypeStruct((cols_all, slice_width + 8, half), BF16)
    far = call(
        functools.partial(target_body, count_data, 1, 1), packed, 4, strips, name="targets_far"
    )(parts, factor, expd, data_all)
    far = swapped(far)
    mine, mass = call(
        functools.partial(target_body, count_data, 0, 1),
        (vmem((cols_all, slice_width, half), F32), jax.ShapeDtypeStruct((half // 128, 128), F32)),
        4, strips, name="targets_own",
    )(parts, factor, expd, data_all)
    pieces = call(pack_body, packed, 3, name="pack")(mine, mass, far)
    got = lax.all_to_all(pieces, COL, 0, 0, tiled=True)
    out = call(finish_body, jax.ShapeDtypeStruct((slice_width, half), BF16), 1, name="finish")(got)
    return out.T


def solution(mesh):
    rows, cols = mesh.devices.shape
    parts = (rows // (XS * CORES), XS, CORES, cols // 2, 2)
    row_split = ("z", "x", "c")
    split = jax.sharding.Mesh(mesh.devices.reshape(parts), row_split + COL)
    return jax.shard_map(
        on_device,
        mesh=split,
        in_specs=(P(row_split, COL), P(COL + row_split, None)),
        out_specs=P(row_split, COL),
        check_vma=False,
    )
```

```python
import functools
import math

import jax
import jax.numpy as jnp
from jax import lax
from jax.experimental import pallas as pl
from jax.experimental.pallas import tpu as pltpu
from jax.sharding import PartitionSpec as P

ITERS = 4
EPS = 0.01
CORES, XS = 2, 4
COL = ("yh", "yl")
SHIFT = 24.0
SCALE = 2.0**48
F32, BF16 = jnp.float32, jnp.bfloat16
VM = pl.BlockSpec(memory_space=pltpu.VMEM)


def params(mib):
    return pltpu.CompilerParams(vmem_limit_bytes=mib * 2**20)


def in_vmem(shape, dtype):
    return pltpu.VMEM(shape, dtype)


def call(body, outs, count, scratch=(), mib=32, name=None):
    return pl.pallas_call(
        body,
        out_shape=outs,
        in_specs=[VM] * count,
        out_specs=jax.tree.map(lambda _: VM, outs, is_leaf=lambda o: hasattr(o, "dtype")),
        scratch_shapes=list(scratch),
        compiler_params=params(mib),
        name=name,
    )


def three(val):
    high = val.astype(BF16).astype(F32)
    mid = (val - high).astype(BF16).astype(F32)
    return high, mid, val - high - mid


def lanes_to_rows(vec, out_ref):
    square = (128, 128)
    on_diagonal = lax.broadcasted_iota(jnp.int32, square, 0) == lax.broadcasted_iota(jnp.int32, square, 1)
    ones = jnp.ones((3 * 128, 128), BF16)
    for r in range(vec.shape[0]):
        pieces = [
            jnp.where(on_diagonal, jnp.broadcast_to(piece, square), 0.0).astype(BF16)
            for piece in three(vec[r : r + 1, :])
        ]
        out_ref[r * 128 : (r + 1) * 128, :] = jnp.dot(
            jnp.concatenate(pieces, axis=1), ones, preferred_element_type=F32
        )


def rows_to_lanes(ref):
    ones = jnp.ones((8, 3 * 128), BF16)
    pieces = jnp.concatenate([piece.astype(BF16) for piece in three(ref[...])], axis=1)
    sums = lax.dot_general(ones, pieces, (((1,), (1,)), ((), ())), preferred_element_type=F32)
    return jnp.concatenate(
        [sums[0:1, r * 128 : (r + 1) * 128] for r in range(ref.shape[0] // 128)], axis=0
    )


def flat(vec):
    return jnp.concatenate([vec[t : t + 1, :] for t in range(vec.shape[0])], axis=1)


def lane_sum(val):
    total = val[:, 0:128]
    for t in range(1, val.shape[1] // 128):
        total = total + val[:, t * 128 : (t + 1) * 128]
    return total


def parts_of(refs):
    parts = []
    for ref in refs:
        if len(ref.shape) == 3:
            parts += [ref[k] for k in range(ref.shape[0])]
        else:
            parts.append(ref[...])
    return parts


def merged(refs):
    parts = parts_of(refs)
    top = functools.reduce(jnp.maximum, parts)
    return top + jnp.log2(sum(jnp.exp2(part - top) for part in parts))


def added(refs):
    return functools.reduce(jnp.add, [part.astype(F32) for part in parts_of(refs)])


def half_at(flip, rows):
    return pl.multiple_of(lax.rem(lax.axis_index("c") + flip, 2) * rows, rows)


def noise_body(parts, out):
    for r in range(out.shape[0] // 128):
        at = slice(r * 128, (r + 1) * 128)
        blocks = [parts[k, :, at].astype(F32).T for k in range(parts.shape[0])]
        out[at, :] = jnp.concatenate(blocks, axis=1).astype(BF16)


def cost_body(noise, data, *refs):
    *before, score, lse, data_sq, rows_sq, part = refs
    rows, depth = noise.shape
    width = 256
    factor = math.log2(math.e) / (depth * EPS)
    contract = (((1,), (1,)), ((), ()))
    for r in range(rows // 128):
        block = noise[r * 128 : (r + 1) * 128, :].astype(F32)
        total = jnp.sum(lane_sum(block * block), axis=1, keepdims=True)
        rows_sq[r * 128 : (r + 1) * 128, :] = jnp.broadcast_to(total * factor, (128, 128))
    for b in range(data.shape[0] // width):
        at = slice(b * width, (b + 1) * width)
        piece = data[at, :]
        places = slice(b * (width // 128), (b + 1) * (width // 128))
        if before:
            data_sq[places, :] = before[1][places, :]
        else:
            wide = piece.astype(F32)
            part[at, :] = lane_sum(wide * wide)
            data_sq[places, :] = rows_to_lanes(part.at[at, :]) * factor
        piece_sq = flat(data_sq[places, :])
        cross = lax.dot_general(noise[...], piece, contract, preferred_element_type=F32)
        sq = jnp.concatenate([rows_sq[...]] * (width // 128), axis=1)
        val = cross * (2.0 * factor) - sq - piece_sq
        score[:, at] = val
        top = jnp.max(val, axis=0, keepdims=True)
        total = jnp.sum(jnp.exp2(val - top), axis=0, keepdims=True)
        sums = top + jnp.log2(total)
        for t in range(width // 128):
            row = slice(b * (width // 128) + t, b * (width // 128) + t + 1)
            lse[row, :] = sums[:, t * 128 : (t + 1) * 128]
    if before:
        lse[...] = merged([lse, before[0]])


def first_row_body(log_data, n, *refs):
    parts, (own, far, expd, peak, lse, part, tops) = refs[:n], refs[n:]
    rows, cols = expd.shape
    half = own.shape[0]
    pot = jnp.broadcast_to(flat(-log_data - merged(parts)), (8, cols))

    def rows_at(base, r):
        return pl.ds(pl.multiple_of(base + r * 8, 8), 8)

    for flip, score in enumerate((own, far)):
        base = half_at(flip, half)

        def find(r, carry):
            val = score[rows_at(0, r), :] + pot
            part[rows_at(base, r), :] = functools.reduce(
                jnp.maximum, [val[:, t * 128 : (t + 1) * 128] for t in range(cols // 128)]
            )
            return carry

        lax.fori_loop(0, half // 8, find, 0, unroll=8)
    high = jnp.concatenate(
        [
            jnp.max(part[r * 128 : (r + 1) * 128, :].T, axis=0, keepdims=True)
            for r in range(rows // 128)
        ],
        axis=0,
    )
    lanes_to_rows(high - SHIFT, tops)
    for flip, score in enumerate((own, far)):
        base = half_at(flip, half)

        def raise_up(r, carry):
            at = rows_at(base, r)
            top = jnp.concatenate([tops[at, :]] * (cols // 128), axis=1)
            e = jnp.exp2((score[rows_at(0, r), :] + pot) - top)
            expd[at, :] = e
            part[at, :] = lane_sum(e)
            return carry

        lax.fori_loop(0, half // 8, raise_up, 0, unroll=8)
    peak[...] = high
    lse[...] = high + (jnp.log2(rows_to_lanes(part)) - SHIFT)


def column_sums(expd, factor, factors, out):
    lanes_to_rows(factor, factors)
    rows, cols = expd.shape
    copies = cols // 128

    def body(r, acc):
        at = pl.ds(pl.multiple_of(r * 8, 8), 8)
        f = factors[at, :]
        return acc + expd[at, :] * jnp.concatenate([f] * copies, axis=1)

    acc = lax.fori_loop(0, rows // 8, body, jnp.zeros((8, cols), F32), unroll=8)
    sums = jnp.sum(acc, axis=0, keepdims=True)
    count, width = out.shape
    rows_out = factors.at[0:count, :]
    for t in range(count):
        rows_out[t : t + 1, :] = sums[:, t * width : (t + 1) * width]
    out[...] = rows_out[...].astype(out.dtype)


def first_col_body(count, n, *refs):
    parts, (peak, expd, out, scale, factors) = refs[:n], refs[n:]
    s = jnp.exp2(peak[...] - merged(parts) + SHIFT)
    scale[...] = s
    column_sums(expd, s * (1.0 / count), factors, out)


def col_body(count, n, *refs):
    parts, (scale, expd, out, *factor, factors) = refs[:n], refs[n:]
    f = scale[...] * ((SCALE / count) / added(parts))
    for ref in factor:
        ref[...] = f
    column_sums(expd, f, factors, out)


def row_body(count, n, *refs):
    parts, (scale, expd, out, part) = refs[:n], refs[n:]
    v = jnp.broadcast_to(flat((SCALE / count) / added(parts)), (8, expd.shape[1]))
    rows = expd.shape[0]

    def body(r, carry):
        at = pl.ds(pl.multiple_of(r * 8, 8), 8)
        part[at, :] = lane_sum(expd[at, :] * v)
        return carry

    lax.fori_loop(0, rows // 8, body, 0, unroll=8)
    out[...] = (rows_to_lanes(part) * scale[...]).astype(out.dtype)


def split_three(mass, deep):
    high = mass.astype(BF16).astype(F32)
    mid = (mass - high).astype(BF16).astype(F32)
    zero = jnp.zeros((deep - 3, mass.shape[1]), F32)
    return jnp.concatenate([high, mid, mass - high - mid, zero], axis=0)


def add_three(tail):
    return tail[0:1, :] + tail[1:2, :] + tail[2:3, :]


def target_body(count, flip, n, *refs):
    parts, (factor, expd, data, out) = refs[:n], refs[n : n + 4]
    *mass, part, factors = refs[n + 4 :]
    v = jnp.broadcast_to(flat((SCALE / count) / added(parts)), (128, expd.shape[1]))
    half, wide = factors.shape[0], expd.shape[1]
    base = half_at(flip, half)
    first = lax.rem(lax.axis_index("c") + flip, 2) * (half // 128)
    lanes_to_rows(factor[pl.ds(first, half // 128), :], factors)
    cols, deep, _ = out.shape
    depth = data.shape[1] // cols
    for r in range(half // 128):
        at = slice(r * 128, (r + 1) * 128)
        f = jnp.concatenate([factors[at, :]] * (wide // 128), axis=1)
        w = expd[pl.ds(pl.multiple_of(base + r * 128, 128), 128), :] * v * f
        total = jnp.sum(lane_sum(w).T, axis=0, keepdims=True)
        part[r : r + 1, :] = total
        block = jnp.dot(w.astype(BF16), data[...], preferred_element_type=F32).T
        tail = [] if mass else [split_three(total, deep - depth)]
        for k in range(cols):
            rows = [block[k * depth : (k + 1) * depth, :]] + tail
            out[k, :, at] = jnp.concatenate(rows, axis=0).astype(out.dtype)
    for ref in mass:
        ref[...] = part[...]


def pack_body(own, mass, far, out):
    depth, deep = own.shape[1], out.shape[1]
    parts = [far[k].astype(F32) for k in range(out.shape[0])]
    tail = split_three(flat(mass[...]) + add_three(parts[0][depth:deep, :]), deep - depth)
    for k, part in enumerate(parts):
        out[k] = jnp.concatenate([own[k] + part[0:depth, :], tail], axis=0).astype(BF16)


def finish_body(parts, out):
    depth = out.shape[0]
    total = functools.reduce(jnp.add, [parts[k].astype(F32) for k in range(parts.shape[0])])
    out[...] = (total[0:depth, :] / add_three(total[depth:, :])).astype(BF16)


def pair_body(here, there, out):
    place = lax.axis_index("yl")
    out[place] = here[...]
    out[1 - place] = there[...]


def spread_body(val, out, sems):
    copies = [pltpu.make_async_copy(val, out.at[k], sems.at[k]) for k in range(out.shape[0])]
    for copy in copies:
        copy.start()
    for copy in copies:
        copy.wait()


def spread(val, count):
    return pl.pallas_call(
        spread_body,
        out_shape=jax.ShapeDtypeStruct((count,) + val.shape, val.dtype),
        in_specs=[VM],
        out_specs=pl.BlockSpec(memory_space=pl.ANY),
        scratch_shapes=[pltpu.SemaphoreType.DMA((count,))],
        compiler_params=params(32),
        name="spread",
    )(val)


def everyone(val, axes):
    count = lax.axis_size(axes)
    copies = jnp.broadcast_to(val[None], (count,) + val.shape)
    return lax.all_to_all(copies, axes, 0, 0, tiled=True)


def swapped(val, axis="c"):
    return lax.ppermute(val, axis, [(0, 1), (1, 0)])


def on_device(noise, data, *, vmem=in_vmem):
    zs, xs, cs, cols_all = (lax.axis_size(a) for a in ("z", "x", "c", COL))
    half, slice_width = noise.shape
    rows = half * cs
    depth = slice_width * cols_all
    wide = data.shape[0] * zs * xs
    count_noise, count_data = float(rows * zs * xs), float(wide * cs * cols_all)
    log_data = math.log2(count_data)
    row_axes, col_axes = ("z", "x"), COL + ("c",)

    here = noise.T
    pair = call(pair_body, jax.ShapeDtypeStruct((2,) + here.shape, BF16), 2, name="pair")(here, swapped(here, "yl"))
    noise_parts = lax.all_gather(pair, "yh", axis=0).reshape(cols_all, slice_width, half)
    copies = spread(data, zs * xs)
    data_all = lax.all_to_all(copies, row_axes, 0, 0, tiled=True).reshape(wide, depth)
    own = call(noise_body, jax.ShapeDtypeStruct((half, depth), BF16), 1, name="noise")(noise_parts)
    far = swapped(own)

    vec_col = jax.ShapeDtypeStruct((wide // 128, 128), F32)
    sent_col = jax.ShapeDtypeStruct((wide // 128, 128), BF16)
    sent_row = jax.ShapeDtypeStruct((rows // 128, 128), BF16)
    vec_row = jax.ShapeDtypeStruct((rows // 128, 128), F32)
    strip = pltpu.VMEM((rows, 128), F32)

    cost_outs = (vmem((half, wide), F32), vec_col, vec_col)
    cost_scratch = [pltpu.VMEM((half, 128), F32), pltpu.VMEM((wide, 128), F32)]
    score_own, *before = call(cost_body, cost_outs, 2, cost_scratch, name="cost_own")(own, data_all)
    score_far, lse, _ = call(cost_body, cost_outs, 4, cost_scratch, name="cost_far")(far, data_all, *before)
    parts = everyone(lse, row_axes)
    expd, peak, lse = call(
        functools.partial(first_row_body, log_data, 1),
        (vmem((rows, wide), F32), vec_row, vec_row), 3, [strip, strip], name="first_rows",
    )(parts, score_own, score_far)
    parts = everyone(lse, col_axes)
    sums, scale = call(
        functools.partial(first_col_body, count_noise, 1),
        (sent_col, vec_row), 3, [strip], name="first_cols",
    )(parts, peak, expd)
    for sweep in range(1, ITERS - 1):
        parts = everyone(sums, row_axes)
        mass = call(
            functools.partial(row_body, count_data, 1), sent_row, 3, [strip], name="rows"
        )(parts, scale, expd)
        parts = everyone(mass, col_axes)
        last = sweep == ITERS - 2
        sums, *factor = call(
            functools.partial(col_body, count_noise, 1),
            (sent_col, vec_row) if last else (sent_col,), 3, [strip], name="cols",
        )(parts, scale, expd)
    (factor,) = factor
    parts = everyone(sums, row_axes)

    strips = [pltpu.VMEM((half // 128, 128), F32), pltpu.VMEM((half, 128), F32)]
    packed = jax.ShapeDtypeStruct((cols_all, slice_width + 8, half), BF16)
    far = call(
        functools.partial(target_body, count_data, 1, 1), packed, 4, strips, name="targets_far"
    )(parts, factor, expd, data_all)
    far = swapped(far)
    mine, mass = call(
        functools.partial(target_body, count_data, 0, 1),
        (vmem((cols_all, slice_width, half), F32), jax.ShapeDtypeStruct((half // 128, 128), F32)),
        4, strips, name="targets_own",
    )(parts, factor, expd, data_all)
    pieces = call(pack_body, packed, 3, name="pack")(mine, mass, far)
    got = lax.all_to_all(pieces, COL, 0, 0, tiled=True)
    out = call(finish_body, jax.ShapeDtypeStruct((slice_width, half), BF16), 1, name="finish")(got)
    return out.T


def solution(mesh):
    rows, cols = mesh.devices.shape
    parts = (rows // (XS * CORES), XS, CORES, cols // 2, 2)
    row_split = ("z", "x", "c")
    split = jax.sharding.Mesh(mesh.devices.reshape(parts), row_split + COL)
    return jax.shard_map(
        on_device,
        mesh=split,
        in_specs=(P(row_split, COL), P(COL + row_split, None)),
        out_specs=P(row_split, COL),
        check_vma=False,
    )
```

```python
import functools
import math

import jax
import jax.numpy as jnp
from jax import lax
from jax.experimental import pallas as pl
from jax.experimental.pallas import tpu as pltpu
from jax.sharding import PartitionSpec as P

ITERS = 4
EPS = 0.01
CORES, XS = 2, 4
COL = ("yh", "yl")
SHIFT = 24.0
SCALE = 2.0**48
F32, BF16 = jnp.float32, jnp.bfloat16
VM = pl.BlockSpec(memory_space=pltpu.VMEM)


def params(mib):
    return pltpu.CompilerParams(vmem_limit_bytes=mib * 2**20)


def in_vmem(shape, dtype):
    return pltpu.VMEM(shape, dtype)


def call(body, outs, count, scratch=(), mib=32, name=None):
    return pl.pallas_call(
        body,
        out_shape=outs,
        in_specs=[VM] * count,
        out_specs=jax.tree.map(lambda _: VM, outs, is_leaf=lambda o: hasattr(o, "dtype")),
        scratch_shapes=list(scratch),
        compiler_params=params(mib),
        name=name,
    )


def lanes_to_rows(vec, out_ref):
    for r in range(vec.shape[0]):
        block = jnp.broadcast_to(vec[r : r + 1, :], (128, 128))
        out_ref[r * 128 : (r + 1) * 128, :] = block.T


def rows_to_lanes(ref):
    parts = []
    for r in range(ref.shape[0] // 128):
        parts.append(jnp.sum(ref[r * 128 : (r + 1) * 128, :].T, axis=0, keepdims=True))
    return jnp.concatenate(parts, axis=0)


def flat(vec):
    return jnp.concatenate([vec[t : t + 1, :] for t in range(vec.shape[0])], axis=1)


def lane_sum(val):
    total = val[:, 0:128]
    for t in range(1, val.shape[1] // 128):
        total = total + val[:, t * 128 : (t + 1) * 128]
    return total


def parts_of(refs):
    parts = []
    for ref in refs:
        if len(ref.shape) == 3:
            parts += [ref[k] for k in range(ref.shape[0])]
        else:
            parts.append(ref[...])
    return parts


def merged(refs):
    parts = parts_of(refs)
    top = functools.reduce(jnp.maximum, parts)
    return top + jnp.log2(sum(jnp.exp2(part - top) for part in parts))


def added(refs):
    return functools.reduce(jnp.add, [part.astype(F32) for part in parts_of(refs)])


def half_at(flip, rows):
    return pl.multiple_of(lax.rem(lax.axis_index("c") + flip, 2) * rows, rows)


def noise_body(parts, out):
    for r in range(out.shape[0] // 128):
        at = slice(r * 128, (r + 1) * 128)
        blocks = [parts[k, :, at].astype(F32).T for k in range(parts.shape[0])]
        out[at, :] = jnp.concatenate(blocks, axis=1).astype(BF16)


def cost_body(noise, data, *refs):
    *before, score, lse, data_sq, rows_sq, part = refs
    rows, depth = noise.shape
    width = 256
    factor = math.log2(math.e) / (depth * EPS)
    contract = (((1,), (1,)), ((), ()))
    for r in range(rows // 128):
        block = noise[r * 128 : (r + 1) * 128, :].astype(F32)
        total = jnp.sum(lane_sum(block * block), axis=1, keepdims=True)
        rows_sq[r * 128 : (r + 1) * 128, :] = jnp.broadcast_to(total * factor, (128, 128))
    for b in range(data.shape[0] // width):
        at = slice(b * width, (b + 1) * width)
        piece = data[at, :]
        places = slice(b * (width // 128), (b + 1) * (width // 128))
        if before:
            data_sq[places, :] = before[1][places, :]
        else:
            wide = piece.astype(F32)
            part[at, :] = lane_sum(wide * wide)
            data_sq[places, :] = rows_to_lanes(part.at[at, :]) * factor
        piece_sq = flat(data_sq[places, :])
        cross = lax.dot_general(noise[...], piece, contract, preferred_element_type=F32)
        sq = jnp.concatenate([rows_sq[...]] * (width // 128), axis=1)
        val = cross * (2.0 * factor) - sq - piece_sq
        score[:, at] = val
        top = jnp.max(val, axis=0, keepdims=True)
        total = jnp.sum(jnp.exp2(val - top), axis=0, keepdims=True)
        sums = top + jnp.log2(total)
        for t in range(width // 128):
            row = slice(b * (width // 128) + t, b * (width // 128) + t + 1)
            lse[row, :] = sums[:, t * 128 : (t + 1) * 128]
    if before:
        lse[...] = merged([lse, before[0]])


def first_row_body(log_data, n, *refs):
    parts, (own, far, expd, tops, lse, part) = refs[:n], refs[n:]
    rows, cols = expd.shape
    half = own.shape[0]
    pot = jnp.broadcast_to(flat(-log_data - merged(parts)), (8, cols))

    def rows_at(base, r):
        return pl.ds(pl.multiple_of(base + r * 8, 8), 8)

    for flip, score in enumerate((own, far)):
        base = half_at(flip, half)

        def body(r, carry):
            at = rows_at(base, r)
            val = score[rows_at(0, r), :] + pot
            tiles = [val[:, t * 128 : (t + 1) * 128] for t in range(cols // 128)]
            top = functools.reduce(jnp.maximum, tiles)
            tops[at, :] = top
            low = top - SHIFT
            e = jnp.concatenate([jnp.exp2(tile - low) for tile in tiles], axis=1)
            expd[at, :] = e
            part[at, :] = lane_sum(e)
            return carry

        lax.fori_loop(0, half // 8, body, 0, unroll=8)
    for r in range(rows // 128):
        at = slice(r * 128, (r + 1) * 128)
        turned = tops[at, :].T
        high = jnp.max(turned, axis=0, keepdims=True)
        total = jnp.sum(jnp.exp2(turned - high) * part[at, :].T, axis=0, keepdims=True)
        lse[r : r + 1, :] = high + (jnp.log2(total) - SHIFT)


def column_sums(expd, factors, out, rows_out):
    rows, cols = expd.shape
    copies = cols // 128

    def body(r, acc):
        at = pl.ds(pl.multiple_of(r * 8, 8), 8)
        f = factors[at, :]
        return acc + expd[at, :] * jnp.concatenate([f] * copies, axis=1)

    acc = lax.fori_loop(0, rows // 8, body, jnp.zeros((8, cols), F32), unroll=8)
    sums = jnp.sum(acc, axis=0, keepdims=True)
    count, width = out.shape
    for t in range(count):
        rows_out[t : t + 1, :] = sums[:, t * width : (t + 1) * width]
    out[...] = rows_out[...].astype(out.dtype)


def first_col_body(count, n, *refs):
    parts, (tops, expd, out, scale, factors, rows_out) = refs[:n], refs[n:]
    lanes_to_rows(merged(parts) - SHIFT, factors)
    s = jnp.exp2(tops[...] - factors[...])
    scale[...] = s
    factors[...] = s * (1.0 / count)
    column_sums(expd, factors, out, rows_out)


def col_body(count, n, *refs):
    parts, (scale, expd, out, factors, rows_out) = refs[:n], refs[n:]
    lanes_to_rows((SCALE / count) / added(parts), factors)
    factors[...] = factors[...] * scale[...]
    column_sums(expd, factors, out, rows_out)


def row_body(count, n, *refs):
    parts, (scale, expd, out, part) = refs[:n], refs[n:]
    v = jnp.broadcast_to(flat((SCALE / count) / added(parts)), (8, expd.shape[1]))
    rows = expd.shape[0]

    def body(r, carry):
        at = pl.ds(pl.multiple_of(r * 8, 8), 8)
        part[at, :] = lane_sum(expd[at, :] * v) * scale[at, :]
        return carry

    lax.fori_loop(0, rows // 8, body, 0, unroll=8)
    out[...] = rows_to_lanes(part).astype(out.dtype)


def split_three(mass, deep):
    high = mass.astype(BF16).astype(F32)
    mid = (mass - high).astype(BF16).astype(F32)
    zero = jnp.zeros((deep - 3, mass.shape[1]), F32)
    return jnp.concatenate([high, mid, mass - high - mid, zero], axis=0)


def add_three(tail):
    return tail[0:1, :] + tail[1:2, :] + tail[2:3, :]


def target_body(count, flip, n, *refs):
    parts, (factor, expd, data, out) = refs[:n], refs[n : n + 4]
    *mass, part = refs[n + 4 :]
    v = jnp.broadcast_to(flat((SCALE / count) / added(parts)), (128, expd.shape[1]))
    half, wide = expd.shape[0] // 2, expd.shape[1]
    base = half_at(flip, half)
    cols, deep, _ = out.shape
    depth = data.shape[1] // cols
    for r in range(half // 128):
        at = slice(r * 128, (r + 1) * 128)
        rows_here = pl.ds(pl.multiple_of(base + r * 128, 128), 128)
        f = jnp.concatenate([factor[rows_here, :]] * (wide // 128), axis=1)
        w = expd[rows_here, :] * v * f
        total = jnp.sum(lane_sum(w).T, axis=0, keepdims=True)
        part[r : r + 1, :] = total
        block = jnp.dot(w.astype(BF16), data[...], preferred_element_type=F32).T
        tail = [] if mass else [split_three(total, deep - depth)]
        for k in range(cols):
            rows = [block[k * depth : (k + 1) * depth, :]] + tail
            out[k, :, at] = jnp.concatenate(rows, axis=0).astype(out.dtype)
    for ref in mass:
        ref[...] = part[...]


def pack_body(own, mass, far, out):
    depth, deep = own.shape[1], out.shape[1]
    parts = [far[k].astype(F32) for k in range(out.shape[0])]
    tail = split_three(flat(mass[...]) + add_three(parts[0][depth:deep, :]), deep - depth)
    for k, part in enumerate(parts):
        out[k] = jnp.concatenate([own[k] + part[0:depth, :], tail], axis=0).astype(BF16)


def finish_body(parts, out):
    depth = out.shape[0]
    total = functools.reduce(jnp.add, [parts[k].astype(F32) for k in range(parts.shape[0])])
    out[...] = (total[0:depth, :] / add_three(total[depth:, :])).astype(BF16)


def pair_body(here, there, out):
    place = lax.axis_index("yl")
    out[place] = here[...]
    out[1 - place] = there[...]


def spread_body(val, out):
    for k in range(out.shape[0]):
        out[k] = val[...]


def everyone(val, axes):
    count = lax.axis_size(axes)
    copies = jnp.broadcast_to(val[None], (count,) + val.shape)
    return lax.all_to_all(copies, axes, 0, 0, tiled=True)


def swapped(val, axis="c"):
    return lax.ppermute(val, axis, [(0, 1), (1, 0)])


def on_device(noise, data, *, vmem=in_vmem):
    zs, xs, cs, cols_all = (lax.axis_size(a) for a in ("z", "x", "c", COL))
    half, slice_width = noise.shape
    rows = half * cs
    depth = slice_width * cols_all
    wide = data.shape[0] * zs * xs
    count_noise, count_data = float(rows * zs * xs), float(wide * cs * cols_all)
    log_data = math.log2(count_data)
    row_axes, col_axes = ("z", "x"), COL + ("c",)

    here = noise.T
    pair = call(pair_body, jax.ShapeDtypeStruct((2,) + here.shape, BF16), 2, name="pair")(here, swapped(here, "yl"))
    noise_parts = lax.all_gather(pair, "yh", axis=0).reshape(cols_all, slice_width, half)
    copies = call(spread_body, vmem((zs * xs,) + data.shape, BF16), 1, name="spread")(data)
    data_all = lax.all_to_all(copies, row_axes, 0, 0, tiled=True).reshape(wide, depth)
    own = call(noise_body, jax.ShapeDtypeStruct((half, depth), BF16), 1, name="noise")(noise_parts)
    far = swapped(own)

    vec_col = jax.ShapeDtypeStruct((wide // 128, 128), F32)
    sent_col = jax.ShapeDtypeStruct((wide // 128, 128), BF16)
    sent_row = jax.ShapeDtypeStruct((rows // 128, 128), BF16)
    vec_row = jax.ShapeDtypeStruct((rows // 128, 128), F32)
    strip = pltpu.VMEM((rows, 128), F32)

    cost_outs = (vmem((half, wide), F32), vec_col, vec_col)
    cost_scratch = [pltpu.VMEM((half, 128), F32), pltpu.VMEM((wide, 128), F32)]
    score_own, *before = call(cost_body, cost_outs, 2, cost_scratch, name="cost_own")(own, data_all)
    score_far, lse, _ = call(cost_body, cost_outs, 4, cost_scratch, name="cost_far")(far, data_all, *before)
    parts = everyone(lse, row_axes)
    by_lane = jax.ShapeDtypeStruct((rows, 128), F32)
    small = pltpu.VMEM((wide // 128, 128), F32)
    expd, tops, lse = call(
        functools.partial(first_row_body, log_data, 1),
        (vmem((rows, wide), F32), by_lane, vec_row), 3, [strip], name="first_rows",
    )(parts, score_own, score_far)
    parts = everyone(lse, col_axes)
    sums, scale = call(
        functools.partial(first_col_body, count_noise, 1),
        (sent_col, by_lane), 3, [strip, small], name="first_cols",
    )(parts, tops, expd)
    for sweep in range(1, ITERS - 1):
        parts = everyone(sums, row_axes)
        mass = call(
            functools.partial(row_body, count_data, 1), sent_row, 3, [strip], name="rows"
        )(parts, scale, expd)
        parts = everyone(mass, col_axes)
        last = sweep == ITERS - 2
        sums, *factor = call(
            functools.partial(col_body, count_noise, 1),
            (sent_col, by_lane) if last else (sent_col,),
            3, [small] if last else [strip, small], name="cols",
        )(parts, scale, expd)
    (factor,) = factor
    parts = everyone(sums, row_axes)

    strips = [pltpu.VMEM((half // 128, 128), F32)]
    packed = jax.ShapeDtypeStruct((cols_all, slice_width + 8, half), BF16)
    far = call(
        functools.partial(target_body, count_data, 1, 1), packed, 4, strips, name="targets_far"
    )(parts, factor, expd, data_all)
    far = swapped(far)
    mine, mass = call(
        functools.partial(target_body, count_data, 0, 1),
        (vmem((cols_all, slice_width, half), F32), jax.ShapeDtypeStruct((half // 128, 128), F32)),
        4, strips, name="targets_own",
    )(parts, factor, expd, data_all)
    pieces = call(pack_body, packed, 3, name="pack")(mine, mass, far)
    got = lax.all_to_all(pieces, COL, 0, 0, tiled=True)
    out = call(finish_body, jax.ShapeDtypeStruct((slice_width, half), BF16), 1, name="finish")(got)
    return out.T


def solution(mesh):
    rows, cols = mesh.devices.shape
    parts = (rows // (XS * CORES), XS, CORES, cols // 2, 2)
    row_split = ("z", "x", "c")
    split = jax.sharding.Mesh(mesh.devices.reshape(parts), row_split + COL)
    return jax.shard_map(
        on_device,
        mesh=split,
        in_specs=(P(row_split, COL), P(COL + row_split, None)),
        out_specs=P(row_split, COL),
        check_vma=False,
    )
```

```python
import functools
import math

import jax
import jax.numpy as jnp
from jax import lax
from jax.experimental import pallas as pl
from jax.experimental.pallas import tpu as pltpu
from jax.sharding import PartitionSpec as P

ITERS = 4
EPS = 0.01
CORES, XS = 2, 4
COL = ("yh", "yl")
SHIFT = 24.0
SCALE = 2.0**48
F32, BF16 = jnp.float32, jnp.bfloat16
VM = pl.BlockSpec(memory_space=pltpu.VMEM)


def params(mib):
    return pltpu.CompilerParams(vmem_limit_bytes=mib * 2**20)


def in_vmem(shape, dtype):
    return pltpu.VMEM(shape, dtype)


def call(body, outs, count, scratch=(), mib=32, name=None):
    return pl.pallas_call(
        body,
        out_shape=outs,
        in_specs=[VM] * count,
        out_specs=jax.tree.map(lambda _: VM, outs, is_leaf=lambda o: hasattr(o, "dtype")),
        scratch_shapes=list(scratch),
        compiler_params=params(mib),
        name=name,
    )


def lanes_to_rows(vec, out_ref):
    for r in range(vec.shape[0]):
        block = jnp.broadcast_to(vec[r : r + 1, :], (128, 128))
        out_ref[r * 128 : (r + 1) * 128, :] = block.T


def rows_to_lanes(ref):
    parts = []
    for r in range(ref.shape[0] // 128):
        parts.append(jnp.sum(ref[r * 128 : (r + 1) * 128, :].T, axis=0, keepdims=True))
    return jnp.concatenate(parts, axis=0)


def flat(vec):
    return jnp.concatenate([vec[t : t + 1, :] for t in range(vec.shape[0])], axis=1)


def lane_sum(val):
    total = val[:, 0:128]
    for t in range(1, val.shape[1] // 128):
        total = total + val[:, t * 128 : (t + 1) * 128]
    return total


def parts_of(refs):
    parts = []
    for ref in refs:
        if len(ref.shape) == 3:
            parts += [ref[k] for k in range(ref.shape[0])]
        else:
            parts.append(ref[...])
    return parts


def merged(refs):
    parts = parts_of(refs)
    top = functools.reduce(jnp.maximum, parts)
    return top + jnp.log2(sum(jnp.exp2(part - top) for part in parts))


def added(refs):
    return functools.reduce(jnp.add, [part.astype(F32) for part in parts_of(refs)])


def half_at(flip, rows):
    return pl.multiple_of(lax.rem(lax.axis_index("c") + flip, 2) * rows, rows)


def noise_body(parts, out):
    for r in range(out.shape[0] // 128):
        at = slice(r * 128, (r + 1) * 128)
        blocks = [parts[k, :, at].astype(F32).T for k in range(parts.shape[0])]
        out[at, :] = jnp.concatenate(blocks, axis=1).astype(BF16)


def cost_body(noise, data, *refs):
    *before, score, lse, data_sq, rows_sq, part = refs
    rows, depth = noise.shape
    width = 256
    factor = math.log2(math.e) / (depth * EPS)
    contract = (((1,), (1,)), ((), ()))
    for r in range(rows // 128):
        block = noise[r * 128 : (r + 1) * 128, :].astype(F32)
        total = jnp.sum(lane_sum(block * block), axis=1, keepdims=True)
        rows_sq[r * 128 : (r + 1) * 128, :] = jnp.broadcast_to(total * factor, (128, 128))
    for b in range(data.shape[0] // width):
        at = slice(b * width, (b + 1) * width)
        piece = data[at, :]
        places = slice(b * (width // 128), (b + 1) * (width // 128))
        if before:
            data_sq[places, :] = before[1][places, :]
        else:
            wide = piece.astype(F32)
            part[at, :] = lane_sum(wide * wide)
            data_sq[places, :] = rows_to_lanes(part.at[at, :]) * factor
        piece_sq = flat(data_sq[places, :])
        cross = lax.dot_general(noise[...], piece, contract, preferred_element_type=F32)
        sq = jnp.concatenate([rows_sq[...]] * (width // 128), axis=1)
        val = cross * (2.0 * factor) - sq - piece_sq
        score[:, at] = val
        top = jnp.max(val, axis=0, keepdims=True)
        total = jnp.sum(jnp.exp2(val - top), axis=0, keepdims=True)
        sums = top + jnp.log2(total)
        for t in range(width // 128):
            row = slice(b * (width // 128) + t, b * (width // 128) + t + 1)
            lse[row, :] = sums[:, t * 128 : (t + 1) * 128]
    if before:
        lse[...] = merged([lse, before[0]])


def first_row_body(log_data, n, *refs):
    parts, (own, far, expd, tops, lse, part) = refs[:n], refs[n:]
    rows, cols = expd.shape
    half = own.shape[0]
    pot = jnp.broadcast_to(flat(-log_data - merged(parts)), (16, cols))

    def rows_at(base, r):
        return pl.ds(pl.multiple_of(base + r * 16, 16), 16)

    for flip, score in enumerate((own, far)):
        base = half_at(flip, half)

        def body(r, carry):
            at = rows_at(base, r)
            val = score[rows_at(0, r), :] + pot
            tiles = [val[:, t * 128 : (t + 1) * 128] for t in range(cols // 128)]
            top = functools.reduce(jnp.maximum, tiles)
            tops[at, :] = top
            low = top - SHIFT
            e = jnp.concatenate([jnp.exp2(tile - low) for tile in tiles], axis=1)
            expd[at, :] = e.astype(BF16)
            part[at, :] = lane_sum(e)
            return carry

        lax.fori_loop(0, half // 16, body, 0, unroll=4)
    for r in range(rows // 128):
        at = slice(r * 128, (r + 1) * 128)
        turned = tops[at, :].T
        high = jnp.max(turned, axis=0, keepdims=True)
        total = jnp.sum(jnp.exp2(turned - high) * part[at, :].T, axis=0, keepdims=True)
        lse[r : r + 1, :] = high + (jnp.log2(total) - SHIFT)


def column_sums(expd, factors, out, rows_out):
    rows, cols = expd.shape
    copies = cols // 128

    def body(r, acc):
        at = pl.ds(pl.multiple_of(r * 16, 16), 16)
        f = factors[at, :]
        terms = expd[at, :].astype(F32) * jnp.concatenate([f] * copies, axis=1)
        return acc + (terms[0:8, :] + terms[8:16, :])

    acc = lax.fori_loop(0, rows // 16, body, jnp.zeros((8, cols), F32), unroll=4)
    sums = jnp.sum(acc, axis=0, keepdims=True)
    count, width = out.shape
    for t in range(count):
        rows_out[t : t + 1, :] = sums[:, t * width : (t + 1) * width]
    out[...] = rows_out[...].astype(out.dtype)


def first_col_body(count, n, *refs):
    parts, (tops, expd, out, scale, factors, rows_out) = refs[:n], refs[n:]
    lanes_to_rows(merged(parts) - SHIFT, factors)
    s = jnp.exp2(tops[...] - factors[...])
    scale[...] = s
    factors[...] = s * (1.0 / count)
    column_sums(expd, factors, out, rows_out)


def col_body(count, n, *refs):
    parts, (scale, expd, out, factors, rows_out) = refs[:n], refs[n:]
    lanes_to_rows((SCALE / count) / added(parts), factors)
    factors[...] = factors[...] * scale[...]
    column_sums(expd, factors, out, rows_out)


def row_body(count, n, *refs):
    parts, (scale, expd, out, part) = refs[:n], refs[n:]
    v = jnp.broadcast_to(flat((SCALE / count) / added(parts)), (16, expd.shape[1]))
    rows = expd.shape[0]

    def body(r, carry):
        at = pl.ds(pl.multiple_of(r * 16, 16), 16)
        part[at, :] = lane_sum(expd[at, :].astype(F32) * v) * scale[at, :]
        return carry

    lax.fori_loop(0, rows // 16, body, 0, unroll=4)
    out[...] = rows_to_lanes(part).astype(out.dtype)


def split_three(mass, deep):
    high = mass.astype(BF16).astype(F32)
    mid = (mass - high).astype(BF16).astype(F32)
    zero = jnp.zeros((deep - 3, mass.shape[1]), F32)
    return jnp.concatenate([high, mid, mass - high - mid, zero], axis=0)


def add_three(tail):
    return tail[0:1, :] + tail[1:2, :] + tail[2:3, :]


def target_body(count, flip, n, *refs):
    parts, (factor, expd, data, out) = refs[:n], refs[n : n + 4]
    *mass, part = refs[n + 4 :]
    v = jnp.broadcast_to(flat((SCALE / count) / added(parts)), (128, expd.shape[1]))
    half, wide = expd.shape[0] // 2, expd.shape[1]
    base = half_at(flip, half)
    cols, deep, _ = out.shape
    depth = data.shape[1] // cols
    for r in range(half // 128):
        at = slice(r * 128, (r + 1) * 128)
        rows_here = pl.ds(pl.multiple_of(base + r * 128, 128), 128)
        f = jnp.concatenate([factor[rows_here, :]] * (wide // 128), axis=1)
        w = expd[rows_here, :].astype(F32) * v * f
        total = jnp.sum(lane_sum(w).T, axis=0, keepdims=True)
        part[r : r + 1, :] = total
        block = jnp.dot(w.astype(BF16), data[...], preferred_element_type=F32).T
        tail = [] if mass else [split_three(total, deep - depth)]
        for k in range(cols):
            rows = [block[k * depth : (k + 1) * depth, :]] + tail
            out[k, :, at] = jnp.concatenate(rows, axis=0).astype(out.dtype)
    for ref in mass:
        ref[...] = part[...]


def pack_body(own, mass, far, out):
    depth, deep = own.shape[1], out.shape[1]
    parts = [far[k].astype(F32) for k in range(out.shape[0])]
    tail = split_three(flat(mass[...]) + add_three(parts[0][depth:deep, :]), deep - depth)
    for k, part in enumerate(parts):
        out[k] = jnp.concatenate([own[k] + part[0:depth, :], tail], axis=0).astype(BF16)


def finish_body(parts, out):
    depth = out.shape[0]
    total = functools.reduce(jnp.add, [parts[k].astype(F32) for k in range(parts.shape[0])])
    out[...] = (total[0:depth, :] / add_three(total[depth:, :])).astype(BF16)


def pair_body(here, there, out):
    place = lax.axis_index("yl")
    out[place] = here[...]
    out[1 - place] = there[...]


def spread_body(val, out):
    for k in range(out.shape[0]):
        out[k] = val[...]


def everyone(val, axes):
    count = lax.axis_size(axes)
    copies = jnp.broadcast_to(val[None], (count,) + val.shape)
    return lax.all_to_all(copies, axes, 0, 0, tiled=True)


def swapped(val, axis="c"):
    return lax.ppermute(val, axis, [(0, 1), (1, 0)])


def on_device(noise, data, *, vmem=in_vmem):
    zs, xs, cs, cols_all = (lax.axis_size(a) for a in ("z", "x", "c", COL))
    half, slice_width = noise.shape
    rows = half * cs
    depth = slice_width * cols_all
    wide = data.shape[0] * zs * xs
    count_noise, count_data = float(rows * zs * xs), float(wide * cs * cols_all)
    log_data = math.log2(count_data)
    row_axes, col_axes = ("z", "x"), COL + ("c",)

    here = noise.T
    pair = call(pair_body, jax.ShapeDtypeStruct((2,) + here.shape, BF16), 2, name="pair")(here, swapped(here, "yl"))
    noise_parts = lax.all_gather(pair, "yh", axis=0).reshape(cols_all, slice_width, half)
    copies = call(spread_body, vmem((zs * xs,) + data.shape, BF16), 1, name="spread")(data)
    data_all = lax.all_to_all(copies, row_axes, 0, 0, tiled=True).reshape(wide, depth)
    own = call(noise_body, jax.ShapeDtypeStruct((half, depth), BF16), 1, name="noise")(noise_parts)
    far = swapped(own)

    vec_col = jax.ShapeDtypeStruct((wide // 128, 128), F32)
    sent_col = jax.ShapeDtypeStruct((wide // 128, 128), BF16)
    sent_row = jax.ShapeDtypeStruct((rows // 128, 128), BF16)
    vec_row = jax.ShapeDtypeStruct((rows // 128, 128), F32)
    strip = pltpu.VMEM((rows, 128), F32)

    cost_outs = (vmem((half, wide), F32), vec_col, vec_col)
    cost_scratch = [pltpu.VMEM((half, 128), F32), pltpu.VMEM((wide, 128), F32)]
    score_own, *before = call(cost_body, cost_outs, 2, cost_scratch, name="cost_own")(own, data_all)
    score_far, lse, _ = call(cost_body, cost_outs, 4, cost_scratch, name="cost_far")(far, data_all, *before)
    parts = everyone(lse, row_axes)
    by_lane = jax.ShapeDtypeStruct((rows, 128), F32)
    small = pltpu.VMEM((wide // 128, 128), F32)
    expd, tops, lse = call(
        functools.partial(first_row_body, log_data, 1),
        (vmem((rows, wide), BF16), by_lane, vec_row), 3, [strip], name="first_rows",
    )(parts, score_own, score_far)
    parts = everyone(lse, col_axes)
    sums, scale = call(
        functools.partial(first_col_body, count_noise, 1),
        (sent_col, by_lane), 3, [strip, small], name="first_cols",
    )(parts, tops, expd)
    for sweep in range(1, ITERS - 1):
        parts = everyone(sums, row_axes)
        mass = call(
            functools.partial(row_body, count_data, 1), sent_row, 3, [strip], name="rows"
        )(parts, scale, expd)
        parts = everyone(mass, col_axes)
        last = sweep == ITERS - 2
        sums, *factor = call(
            functools.partial(col_body, count_noise, 1),
            (sent_col, by_lane) if last else (sent_col,),
            3, [small] if last else [strip, small], name="cols",
        )(parts, scale, expd)
    (factor,) = factor
    parts = everyone(sums, row_axes)

    strips = [pltpu.VMEM((half // 128, 128), F32)]
    packed = jax.ShapeDtypeStruct((cols_all, slice_width + 8, half), BF16)
    far = call(
        functools.partial(target_body, count_data, 1, 1), packed, 4, strips, name="targets_far"
    )(parts, factor, expd, data_all)
    far = swapped(far)
    mine, mass = call(
        functools.partial(target_body, count_data, 0, 1),
        (vmem((cols_all, slice_width, half), F32), jax.ShapeDtypeStruct((half // 128, 128), F32)),
        4, strips, name="targets_own",
    )(parts, factor, expd, data_all)
    pieces = call(pack_body, packed, 3, name="pack")(mine, mass, far)
    got = lax.all_to_all(pieces, COL, 0, 0, tiled=True)
    out = call(finish_body, jax.ShapeDtypeStruct((slice_width, half), BF16), 1, name="finish")(got)
    return out.T


def solution(mesh):
    rows, cols = mesh.devices.shape
    parts = (rows // (XS * CORES), XS, CORES, cols // 2, 2)
    row_split = ("z", "x", "c")
    split = jax.sharding.Mesh(mesh.devices.reshape(parts), row_split + COL)
    return jax.shard_map(
        on_device,
        mesh=split,
        in_specs=(P(row_split, COL), P(COL + row_split, None)),
        out_specs=P(row_split, COL),
        check_vma=False,
    )
```
